32 devices in a mesh: dp: 8 (over z, y), mp: 4 (over x, core).
Axes of the slice: x: 2, y: 2, z: 4, core: 2. Of those that a mesh axis runs over, the one named last changes fastest.
Arguments:
- passages_in: bfloat16 [18432, 768], P(('dp', 'mp')), may hold values from -6 to 6
- queries: bfloat16 [16, 32, 128], P('dp', 'mp'), may hold values from -0.5390625 to 0.5390625
- w_qkv: bfloat16 [2, 768, 3, 768], P(None, None, None, 'mp'), may hold values from -0.21875 to 0.21875
- b_qv: float32 [2, 2, 768], P(None, None, 'mp'), may hold values from -3 to 3
- w_out: bfloat16 [2, 768, 768], P(None, 'mp'), may hold values from -2.5 to 2.5
- b_out: float32 [2, 768], replicated, may hold values from -3 to 3
- ln_gain: float32 [2, 2, 768], replicated, may hold values from 0.5 to 1.5
- ln_shift: float32 [2, 2, 768], replicated, may hold values from -2 to 2
- w_up: bfloat16 [2, 768, 3072], P(None, None, 'mp'), may hold values from -0.21875 to 0.21875
- b_up: bfloat16 [2, 3072], P(None, 'mp'), may hold values from -3 to 3
- w_down: bfloat16 [2, 3072, 768], P(None, 'mp'), may hold values from -0.15625 to 0.15625
- b_down: float32 [2, 768], replicated, may hold values from -3 to 3
- w_proj: bfloat16 [768, 128], replicated, may hold values from -0.21875 to 0.21875
- lengths: int32 [16, 8], P('dp'), may hold values from 1 to 1024, 1152 in all within a row
- passage_group: int32 [16, 8], P('dp'), may hold values from 0 to 7, as said below
- positive: int32 [16], replicated, may hold values from 0 to 127, as said below
Outputs:
- query_loss: float32 [16], P('dp')
- input_grad: float32 [18432, 768], P(('dp', 'mp'))
- query_grad: float32 [16, 32, 128], P('dp', 'mp')
- g_wqkv: float32 [2, 768, 3, 768], P(None, None, None, 'mp')
- g_bqv: float32 [2, 2, 768], P(None, None, 'mp')
- g_wout: float32 [2, 768, 768], P(None, 'mp')
- g_bout: float32 [2, 768], replicated
- g_lngain: float32 [2, 2, 768], replicated
- g_lnshift: float32 [2, 2, 768], replicated
- g_wup: float32 [2, 768, 3072], P(None, None, 'mp')
- g_bup: float32 [2, 3072], P(None, 'mp')
- g_wdown: float32 [2, 3072, 768], P(None, 'mp')
- g_bdown: float32 [2, 768], replicated
- g_wproj: float32 [768, 128], replicated
The draws below stay inside these ranges and needn't reach their ends.
Inputs may be any that keep to these rules, and one draw needn't show every extreme that they name: `lengths`: each row sums to 1152; every row has one passage of exactly 1024 tokens. `passage_group`: every group is named by exactly 16 passages. positive[q] is the global passage index (row-major over passage_group) of a passage of group q // 2.
All inputs are finite; a program needn't handle non-finite values.
Results may differ from the reference program's by a relative error of at most 0.025.
Values may be sent and summed in bfloat16 or wider, within the bound.
No kernel may reach another device: no remote copies, remote signals or barrier semaphores. Data moves between devices by JAX's collectives and lax.ppermute only.
A program may use at most 320 MiB of HBM per device.

```python
import math
import jax
import jax.numpy as jnp
import numpy as np
from jax import lax

D = 768
HEADS = 12
HEAD = 64
FF = 3072
DIM = 128
QLEN = 32
QG = 2
LAYERS = 2
MICRO = 2
P_MB = 8
TOK_MB = 1152
LONGEST = 1024
TOKENS = 18432
NQ = 16
N_DP = 8


def shared_order(key):
    return jax.random.permutation(key, N_DP * MICRO * P_MB)


def draw_passage_group(key, part):
    shuffle = shared_order(key)
    return (shuffle // (MICRO * P_MB)).astype(jnp.int32).reshape(N_DP * MICRO, P_MB)


def draw_positive(key, part):
    shuffle = shared_order(key)
    key = jax.random.fold_in(key, 7)
    inverse = jnp.argsort(shuffle)
    pick_slot = jax.random.randint(key, (N_DP * QG,), 0, MICRO * P_MB)
    slot_ids = jnp.arange(N_DP * QG, dtype=jnp.int32) // QG * (MICRO * P_MB) + pick_slot
    return inverse[slot_ids].astype(jnp.int32)


def level_of(own_key, dims, cuts, smallest, largest):
    level, own = 1.0, jax.random.fold_in(own_key, 6)
    for dim, shards_of in cuts:
        steps = jnp.exp(jax.random.uniform(jax.random.fold_in(own, dim), (shards_of,), jnp.float32, smallest / len(cuts), largest / len(cuts)))
        level = level * jnp.repeat(steps, dims[dim] // shards_of).reshape([-1 if axis == dim else 1 for axis in range(len(dims))])
    return level


def split_up(number_of, total, limit, lean):
    portions = [(1 << 20) // math.isqrt(standing ** lean) + 1 for standing in range(2, number_of + 1)]
    surplus, counts = total - limit - (number_of - 1), [1] * (number_of - 1)
    while surplus > 0:
        movable = [i for i in range(number_of - 1) if counts[i] < limit]
        pool, budget = sum([portions[i] for i in movable]), surplus
        for i in movable:
            addition = min(limit - counts[i], max(1, budget * portions[i] // pool), surplus)
            counts[i] = counts[i] + addition
            surplus = surplus - addition
    return np.array([limit] + counts)


def uneven_parts(stream_key, count, total, most, lean):
    if count == 2:
        one = jax.random.randint(stream_key, (), max(1, total - most), min(most, total - 1) + 1)
        return jnp.stack([one, total - one])
    sizes = jnp.asarray(split_up(count, total, most, lean), jnp.int32)
    twos = (count - 1) // 2
    giver, sink = sizes[1:1 + 2 * twos:2], sizes[2:2 + 2 * twos:2]
    slack = jnp.minimum(giver - 1, most - sink)
    moved = jax.random.randint(jax.random.fold_in(stream_key, 1), (twos,), 0, 1 << 20) % (slack + 1)
    sizes = sizes.at[1:1 + 2 * twos:2].set(giver - moved).at[2:2 + 2 * twos:2].set(sink + moved)
    return sizes[jax.random.permutation(jax.random.fold_in(stream_key, 2), count)]


def scatter_about(own_key, extent, deviation, most, pieces=(), held_as=jnp.bfloat16):
    gain = level_of(own_key, extent, pieces, -0.22, 0.18) if pieces else 1.0
    values = jax.random.normal(own_key, extent, jnp.float32) * deviation * gain
    return jnp.minimum(jnp.maximum(values, -most), most).astype(held_as)


def setup_inputs(seed: int = 0) -> dict:
    streams_of = jax.random.split(jax.random.key(seed), 17)
    return {
        "passages_in": scatter_about(streams_of[0], (TOKENS, D), 1.0, 6.0, ((0, 32),)),
        "queries": scatter_about(streams_of[1], (NQ, QLEN, DIM), 0.09, 0.5390625, ((0, 8), (1, 4))),
        "w_qkv": scatter_about(streams_of[2], (LAYERS, D, 3, D), D ** -0.5, 0.21875, ((3, 4),)),
        "b_qv": scatter_about(streams_of[3], (LAYERS, 2, D), 0.5, 3.0, ((2, 4),), jnp.float32),
        "w_out": scatter_about(streams_of[4], (LAYERS, D, D), (max(D // 128, 1)) ** -0.5, 2.5, ((1, 4),)),
        "b_out": scatter_about(streams_of[5], (LAYERS, D), 0.5, 3.0, (), jnp.float32),
        "ln_gain": jnp.clip(1.0 + 0.1 * jax.random.normal(streams_of[6], (LAYERS, 2, D), jnp.float32), 0.5, 1.5),
        "ln_shift": scatter_about(streams_of[7], (LAYERS, 2, D), 0.3, 2.0, (), jnp.float32),
        "w_up": scatter_about(streams_of[8], (LAYERS, D, FF), D ** -0.5, 0.21875, ((2, 4),)),
        "b_up": scatter_about(streams_of[9], (LAYERS, FF), 0.5, 3.0, ((1, 4),)),
        "w_down": scatter_about(streams_of[10], (LAYERS, FF, D), (FF // 2) ** -0.5, 0.15625, ((1, 4),)),
        "b_down": scatter_about(streams_of[11], (LAYERS, D), 0.5, 3.0, (), jnp.float32),
        "w_proj": scatter_about(streams_of[12], (D, DIM), D ** -0.5, 0.21875),
        "lengths": jax.vmap(lambda own: uneven_parts(own, P_MB, TOK_MB, LONGEST, 2))(jax.random.split(streams_of[13], (N_DP * MICRO))).reshape((N_DP * MICRO, P_MB)).astype(jnp.int32),
        "passage_group": draw_passage_group(jax.random.fold_in(streams_of[16], 71), 0),
        "positive": draw_positive(jax.random.fold_in(streams_of[16], 71), 0),
    }


SHARP = 4.0
TEMPER = 0.2
LN_EPS = 1e-12
UNIT_EPS = 1e-06
MASKED = -1000000000.0
FLOOR = -1e+30
HIGH = lax.Precision.HIGHEST

@jax.custom_vjp
def low(v):
    return lax.optimization_barrier(v.astype(jnp.bfloat16)).astype(jnp.float32)

@jax.custom_vjp
def low_back(v):
    return v

def low_keep(v):
    return (low(v), None)

def low_pass(kept, grad):
    return (grad,)

def back_keep(v):
    return (v, None)

def back_low(kept, grad):
    return (low(grad),)
low.defvjp(low_keep, low_pass)
low_back.defvjp(back_keep, back_low)

def mat_high(left_side, right_side):
    return jnp.dot(left_side, right_side, precision=HIGH)

def layer_norm(norm_in, gain_vec, shift_vec):
    mean_val = lax.optimization_barrier(jnp.mean(norm_in, -1, keepdims=True))
    centered = norm_in - mean_val
    inv_std = lax.rsqrt(lax.optimization_barrier(jnp.mean(centered * centered, -1, keepdims=True)) + LN_EPS)
    return centered * inv_std * gain_vec + shift_vec

def attend_block(packed):
    q_blk, k_blk, v_blk, seg_blk = packed
    q_heads = q_blk.reshape(TOK_MB, HEADS, HEAD)
    k_heads = k_blk.reshape(TOK_MB, HEADS, HEAD)
    v_heads = v_blk.reshape(TOK_MB, HEADS, HEAD)
    scores_blk = jnp.einsum('qhe,khe->hqk', q_heads, k_heads, precision=HIGH) * HEAD ** (-0.5)
    scores_blk = low_back(scores_blk)
    same_seg = seg_blk[:, None] == seg_blk[None, :]
    scores_blk = jnp.where(same_seg[None], scores_blk, MASKED)
    probs = low(jax.nn.softmax(scores_blk, axis=-1))
    out_blk = jnp.einsum('hqk,khe->qhe', probs, v_heads, precision=HIGH)
    return out_blk.reshape(TOK_MB, D)

def forward(param_list, lengths, passage_group, positive):
    states, queries, w_qkv, b_qv, w_out, b_out, ln_gain, ln_shift, w_up, b_up, w_down, b_down, w_proj = param_list
    block_count = N_DP * MICRO
    passage_ends = jnp.cumsum(lengths, 1)
    positions = jnp.arange(TOK_MB, dtype=jnp.int32)
    segments = lax.optimization_barrier(jnp.sum((passage_ends[:, None, :] <= positions[None, :, None]).astype(jnp.int32), 2))
    residual = states
    for layer_at in range(LAYERS):
        x_in = low(residual)
        projected = mat_high(x_in, w_qkv[layer_at].reshape(D, 3 * D))
        q_val = low(low_back(projected[:, :D] + b_qv[layer_at, 0]))
        k_val = low(low_back(projected[:, D:2 * D]))
        v_val = low(low_back(projected[:, 2 * D:] + b_qv[layer_at, 1]))
        attended = lax.map(jax.checkpoint(attend_block), (q_val.reshape(block_count, TOK_MB, D), k_val.reshape(block_count, TOK_MB, D), v_val.reshape(block_count, TOK_MB, D), segments))
        attended = low(low_back(attended.reshape(block_count * TOK_MB, D)))
        branch_one = low_back(mat_high(attended, w_out[layer_at]) + b_out[layer_at])
        y_one = layer_norm(residual + branch_one, ln_gain[layer_at, 0], ln_shift[layer_at, 0])
        pre_act = low_back(mat_high(low(y_one), w_up[layer_at]) + b_up[layer_at])
        hidden = low(jax.nn.gelu(pre_act, approximate=False))
        branch_two = low_back(mat_high(hidden, w_down[layer_at]) + b_down[layer_at])
        residual = layer_norm(y_one + branch_two, ln_gain[layer_at, 1], ln_shift[layer_at, 1])
    embedded = low_back(mat_high(low(residual), w_proj))
    unit_vec = low(embedded * lax.rsqrt(lax.optimization_barrier(jnp.sum(embedded * embedded, -1, keepdims=True)) + UNIT_EPS))
    q_groups = queries.reshape(N_DP, QG * QLEN, DIM)

    def score_block(packed):
        unit_blk, seg_blk, group_blk = packed
        picked = q_groups[group_blk]
        similar = low_back(jnp.einsum('td,pqd->tpq', unit_blk, picked, precision=HIGH))
        owners = (seg_blk[:, None] == jnp.arange(P_MB, dtype=jnp.int32)[None, :]).astype(jnp.float32)
        weights_tok = jnp.exp(SHARP * (similar - 1.0)) * owners[:, :, None]
        return lax.optimization_barrier(jnp.sum(weights_tok, 0))
    totals = lax.map(jax.checkpoint(score_block), (unit_vec.reshape(block_count, TOK_MB, DIM), segments, passage_group))
    totals = totals.reshape(block_count * P_MB, QG * QLEN)
    span_len = lengths.reshape(block_count * P_MB).astype(jnp.float32)
    term_all = (jnp.log(totals) - jnp.log(span_len)[:, None]) / SHARP + 1.0
    logits = lax.optimization_barrier(jnp.sum(term_all.reshape(block_count * P_MB, QG, QLEN), -1)) / TEMPER
    member = passage_group.reshape(block_count * P_MB)[:, None] == jnp.arange(N_DP, dtype=jnp.int32)[None, :]
    spread_logit = jnp.where(member[:, :, None], logits[:, None, :], FLOOR)
    lse_q = jax.nn.logsumexp(spread_logit, axis=0)
    targets = positive.reshape(N_DP, QG)
    aimed_at = logits[targets, jnp.arange(QG, dtype=jnp.int32)[None, :]]
    query_loss = (lse_q - aimed_at).reshape(N_DP * QG)
    return (jnp.sum(query_loss), query_loss)

def reference(passages_in, queries, w_qkv, b_qv, w_out, b_out, ln_gain, ln_shift, w_up, b_up, w_down, b_down, w_proj, lengths, passage_group, positive):
    param_list = tuple((value.astype(jnp.float32) for value in (passages_in, queries, w_qkv, b_qv, w_out, b_out, ln_gain, ln_shift, w_up, b_up, w_down, b_down, w_proj)))

    def loss_of(params_in):
        return forward(params_in, lengths, passage_group, positive)
    total, pull_back, query_loss = jax.vjp(loss_of, param_list, has_aux=True)
    grads, = pull_back(jnp.ones_like(total))
    return (query_loss, grads[0], grads[1], grads[2], grads[3], grads[4], grads[5], grads[6], grads[7], grads[8], grads[9], grads[10], grads[11], grads[12])
```

```python
from types import SimpleNamespace

import jax
import jax.numpy as jnp
from jax import lax
from jax.experimental import pallas as pl
from jax.experimental.pallas import tpu as pltpu
from jax.sharding import PartitionSpec as P

HEAD = 64
LONGEST = 1024
SHARP = 4.0
TEMPER = 0.2
LN_EPS = 1e-12
UNIT_EPS = 1e-06
MASKED = -1000000000.0
FLOOR = -1e30
Q_ROWS = 512
AHEAD = 3
COST = 5000000
TURNS = (1, 2, 3, 1, 3, 4, 2, 1, 3, 4, 0, 2, 1, 3, 4, 2, 3, 0, 1, 4, 2, 3, 2, 3)
VMEM_LIMIT = 40 * 2**20

bf16 = jnp.bfloat16
f32 = jnp.float32
i32 = jnp.int32
HIGH = lax.Precision.HIGHEST
VMEM = pl.BlockSpec(memory_space=pltpu.VMEM)
SMEM = pl.BlockSpec(memory_space=pltpu.SMEM)
HBM = pl.BlockSpec(memory_space=pltpu.HBM)
NEAR, FAR, SCALAR = range(3)


def nn(left_side, right_side):
    return lax.dot_general(
        left_side, right_side, (((1,), (0,)), ((), ())), preferred_element_type=f32
    )


def nt(left_side, right_side):
    return lax.dot_general(
        left_side, right_side, (((1,), (1,)), ((), ())), preferred_element_type=f32
    )


def tn(left_side, right_side):
    return lax.dot_general(
        left_side, right_side, (((0,), (0,)), ((), ())), preferred_element_type=f32
    )


def exact(left_side, right_side, dims=((1,), (0,))):
    return lax.dot_general(
        left_side, right_side, (dims, ((), ())), precision=HIGH, preferred_element_type=f32
    )


def gelu_pair(values):
    size = jnp.abs(values)
    t = 1.0 / (1.0 + (0.3275911 * 0.7071067811865476) * size)
    bell = jnp.exp(-0.5 * values * values)
    poly = t * (
        0.254829592
        + t * (-0.284496736 + t * (1.421413741 + t * (-1.453152027 + t * 1.061405429)))
    )
    tail = 0.5 * poly * bell
    phi = jnp.where(values < 0, tail, 1.0 - tail)
    return values * phi, phi + values * (0.3989422804014327 * bell)


class Fetched:
    def __init__(self, ref, held, sem, line):
        self.copy, self.held, self.line, self.due = pltpu.make_async_copy(ref, held, sem), held, line, True
        line.append(self)

    def begin(self):
        self.line.remove(self)
        self.copy.start()

    def __getitem__(self, at):
        if self.due:
            if self in self.line:
                self.begin()
            if self.line:
                self.line[0].begin()
            self.copy.wait()
            self.due = False
        value = self.held[at]
        return value.reshape(-1, value.shape[-1]) if value.ndim == 3 else value


class Flushed:
    def __init__(self, ref, held, sems, pieces):
        self.ref, self.held, self.sems, self.pieces = ref, held, sems, pieces
        self.copies = []

    def __getitem__(self, at):
        return self.held[at]

    def __setitem__(self, at, value):
        self.held[at] = value

    def flush(self, which=0):
        first, last = self.pieces[which]
        rows = pl.ds(first, last - first)
        copy = pltpu.make_async_copy(self.held.at[rows], self.ref.at[rows], self.sems.at[which])
        copy.start()
        self.copies.append(copy)


def part_shape(shape, part=()):
    if isinstance(part, int):
        return shape[1:]
    return tuple(len(range(*at.indices(size))) for at, size in zip(part, shape)) + shape[len(part) :]


def run(name, body, operands, results, scratch=()):
    spaces = (pltpu.VMEM, pltpu.HBM)
    kinds = [given[0] for given in operands.values()]
    arrays = [
        given[1] if given[0] == SCALAR else pltpu.with_memory_space_constraint(given[1], spaces[given[0]])
        for given in operands.values()
    ]
    parts = [given[2:] for given in operands.values()]
    fetch = [at for at, kind in enumerate(kinds) if kind == FAR]
    made = list(results.values())
    pieces = {}
    for at, (kind, shape, _) in enumerate(made):
        if kind != NEAR:
            pieces[at] = [(0, shape[0])] if kind == FAR else kind
    added = [pltpu.VMEM(part_shape(arrays[at].shape, *parts[at]), arrays[at].dtype) for at in fetch]
    added += [pltpu.VMEM(made[at][1], made[at][2]) for at in pieces]
    added += [pltpu.SemaphoreType.DMA((max(len(fetch), 1),))]
    added += [pltpu.SemaphoreType.DMA((len(rows),)) for rows in pieces.values()]

    def outer(*refs):
        refs = list(refs)
        first = len(refs) - len(added)
        extra, refs = refs[first:], refs[:first]
        sems = extra[len(fetch) + len(pieces) :]
        line = []
        for count, at in enumerate(fetch):
            ref = refs[at].at[parts[at][0]] if parts[at] else refs[at]
            refs[at] = Fetched(ref, extra[count], sems[0].at[count], line)
        for _ in range(min(AHEAD, len(line))):
            line[0].begin()
        outs = []
        for count, (at, rows) in enumerate(pieces.items()):
            out = Flushed(refs[len(operands) + at], extra[len(fetch) + count], sems[1 + count], rows)
            refs[len(operands) + at] = out
            outs.append(out)
        named = SimpleNamespace(scratch=refs[len(operands) + len(results) :])
        for key, ref in zip(list(operands) + list(results), refs):
            setattr(named, key, ref)
        body(named)
        for at in fetch:
            refs[at][0:1]
        for out in outs:
            for copy in out.copies:
                copy.wait()

    given = pl.pallas_call(
        outer,
        out_shape=tuple(spaces[kind != NEAR](shape, dtype) for kind, shape, dtype in made),
        in_specs=[(VMEM, HBM, SMEM)[kind] for kind in kinds],
        out_specs=tuple(VMEM if kind == NEAR else HBM for kind, _, _ in made),
        scratch_shapes=list(scratch) + added,
        compiler_params=pltpu.CompilerParams(vmem_limit_bytes=VMEM_LIMIT),
        cost_estimate=pl.CostEstimate(flops=COST, transcendentals=0, bytes_accessed=0),
        name=name,
    )(*arrays)
    return SimpleNamespace(**dict(zip(results, given)))


def facts(meta, per):
    core, micro = meta[1] % 2, meta[1] // 2
    ends, begin, last = [], 0, 0
    for at in range(per):
        length = meta[2 + micro * per + at]
        begin = begin + jnp.where(length == LONGEST, last, 0)
        last = last + length
        ends.append(last)
    groups = [meta[2 + 2 * per + micro * per + at] for at in range(per)]
    return core, micro, begin, ends, groups


def long_rows(values, half, small):
    return jnp.concatenate([values[0:half], values[half + small : 2 * half + small]], 0)


def small_rows(values, half, small):
    return jnp.concatenate([values[half : half + small], values[2 * half + small :]], 0)


def q_starts(half, small, step):
    return [at for base in (0, half + small) for at in range(base, base + half, step)]


def segment_of(place, ends):
    return sum((place >= end).astype(i32) for end in ends)


def small_same(meta, per, small):
    core, _, begin, ends, _ = facts(meta, per)

    def segments(shape, axis):
        at = lax.broadcasted_iota(i32, shape, axis)
        which = jnp.where(at < small, core, 1 - core)
        place = begin + LONGEST + which * small + jnp.where(at < small, at, at - small)
        total = LONGEST + 2 * small
        return segment_of(jnp.where(place >= total, place - total, place), ends)

    count = 2 * small
    return segments((count, count), 0) == segments((count, count), 1)


def row_places(meta, per, half, small, axis):
    core, _, begin, _, _ = facts(meta, per)
    own = half + small
    at = lax.broadcasted_iota(i32, (2 * own, 1) if axis == 0 else (1, 2 * own), axis)
    which = jnp.where(at < own, core, 1 - core)
    at = jnp.where(at < own, at, at - own)
    place = begin + jnp.where(at < half, which * half + at, LONGEST + which * small + at - half)
    total = LONGEST + 2 * small
    return jnp.where(place >= total, place - total, place)


def row_segments(meta, per, half, small):
    return segment_of(row_places(meta, per, half, small, 0), facts(meta, per)[3])


def chunks(rows):
    step = rows // PIECES
    return [slice(at, at + step) for at in range(0, rows, step)]


PIECES = 4


def both(refs, rows):
    at = rows.start // (rows.stop - rows.start)
    there = (at + PIECES // 2) % PIECES
    return getattr(refs, f"mine{at}")[...].astype(f32) + getattr(refs, f"came{there}")[...].astype(f32)


def parts_in(norm):
    made = {f"mine{at}": (NEAR, value) for at, value in enumerate(norm.mine)}
    return made | {f"came{at}": (NEAR, value) for at, value in enumerate(norm.came)}


def parts_out(rows, model):
    return {f"mine{at}": (NEAR, (rows // PIECES, model), bf16) for at in range(PIECES)}


def parts_of(got):
    return [getattr(got, f"mine{at}") for at in range(PIECES)]


def norm_into(refs, line):
    vecs = refs.vecs[8 * line : 8 * line + 8]
    for rows in chunks(refs.low.held.shape[0]):
        value = refs.base[rows].astype(f32) + (both(refs, rows) + vecs[0:1])
        centered = value - jnp.mean(value, -1, keepdims=True)
        inv_std = lax.rsqrt(jnp.mean(centered * centered, -1, keepdims=True) + LN_EPS)
        normed = centered * inv_std
        made = normed * vecs[1:2] + vecs[2:3]
        if hasattr(refs, "y"):
            refs.y[rows] = made
        refs.low[rows] = made.astype(bf16)
        refs.n[rows] = normed.astype(bf16)
        refs.r[rows] = inv_std
    for ref in (refs.low, refs.n, refs.r):
        ref.flush()
    if hasattr(refs, "y"):
        refs.y.flush()


def norm_results(rows, width, keep=True):
    made = dict(
        low=(FAR, (rows, width), bf16),
        n=(FAR, (rows, width), bf16),
        r=(FAR, (rows, 1), f32),
    )
    return made | (dict(y=(FAR, (rows, width), f32)) if keep else {})


def norm_back_into(refs, line):
    gain = refs.vecs[8 * line : 8 * line + 8][1:2]
    sums = None
    rows_all = refs.n.held.shape[0]
    for rows in chunks(rows_all):
        if hasattr(refs, "grad"):
            grad = refs.grad[rows]
        else:
            grad = refs.base[rows] + both(refs, rows)
        normed = refs.n[rows].astype(f32)
        inner = grad * gain
        made = refs.r[rows] * (
            inner
            - jnp.mean(inner, -1, keepdims=True)
            - normed * jnp.mean(inner * normed, -1, keepdims=True)
        )
        low = made.astype(bf16)
        refs.g[rows] = made
        refs.low[rows] = low
        lines = [
            jnp.sum(value, 0, keepdims=True) for value in (grad * normed, grad, low.astype(f32))
        ]
        sums = lines if sums is None else [a + b for a, b in zip(sums, lines)]
    refs.g.flush()
    refs.low.flush()
    for at, value in enumerate(sums):
        refs.sums[at : at + 1] = value
    refs.sums[3:] = jnp.zeros((5, sums[0].shape[1]), f32)
    refs.sums.flush()


def heads_into(refs, meta, per, line, heads, half, small):
    width = heads * HEAD
    x_ref = refs.low
    bias = refs.units[line : line + 1]
    made = nt(x_ref[...], refs.w_qkv[...])
    refs.q[...] = (made[:, :width] + bias[:, :width]).astype(bf16)
    refs.k[...] = made[:, width : 2 * width].astype(bf16)
    refs.v[...] = (made[:, 2 * width :] + bias[:, width : 2 * width]).astype(bf16)
    for ref in (refs.q, refs.k, refs.v):
        ref.flush()
    scale = HEAD**-0.5
    same = small_same(meta, per, small)
    a_out, lse_out = refs.a, refs.lse
    for head in range(heads):
        cols = slice(head * HEAD, (head + 1) * HEAD)
        line = slice(head, head + 1)
        k_head = refs.k[:, cols]
        v_head = refs.v[:, cols]
        q_head = refs.q[:, cols] * scale
        k_long = long_rows(k_head, half, small)
        v_long_t = long_rows(v_head, half, small).T
        for at in q_starts(half, small, Q_ROWS):
            scores = nt(k_long, q_head[at : at + Q_ROWS])
            top = jnp.max(scores, 0, keepdims=True)
            probs = jnp.exp(scores - top)
            mass = jnp.sum(probs, 0, keepdims=True)
            out = nn(v_long_t, probs.astype(bf16)) / mass
            a_out[at : at + Q_ROWS, cols] = out.T.astype(bf16)
            lse_out[line, at : at + Q_ROWS] = top + jnp.log(mass)
        scores = nt(small_rows(k_head, half, small), small_rows(q_head, half, small))
        scores = jnp.where(same, scores, MASKED)
        top = jnp.max(scores, 0, keepdims=True)
        probs = jnp.exp(scores - top)
        mass = jnp.sum(probs, 0, keepdims=True)
        out = nn(small_rows(v_head, half, small).T, probs.astype(bf16)) / mass
        out = out.T.astype(bf16)
        a_out[half : half + small, cols] = out[:small]
        a_out[2 * half + small :, cols] = out[small:]
        lse = top + jnp.log(mass)
        lse_out[line, half : half + small] = lse[:, :small]
        lse_out[line, 2 * half + small :] = lse[:, small:]
    a_out.flush()
    lse_out.flush()


def heads_results(rows, width):
    made = (FAR, (rows, width), bf16)
    return dict(q=made, k=made, v=made, a=made, lse=(FAR, (8, rows), f32))


def attend_first(meta, per, small, line, x_all, norm, w_qkv, layer, units):
    width = w_qkv.shape[1] // 3
    heads = width // HEAD
    rows, model = (x_all if norm is None else norm.base).shape
    half = rows // 2 - small
    operands = dict(meta=(SCALAR, meta))
    results = {}
    if norm is None:
        operands |= dict(low=(NEAR, x_all))
    else:
        operands |= parts_in(norm) | dict(base=(FAR, norm.base), vecs=(FAR, norm.vecs))
        results = norm_results(rows, model)
    operands |= dict(w_qkv=(FAR, w_qkv, layer), units=(FAR, units))

    def body(refs):
        if norm is not None:
            norm_into(refs, norm.line)
        heads_into(refs, refs.meta, per, line, heads, half, small)

    return run("attend", body, operands, results | heads_results(rows, width))


def attend_second(meta, per, small, line, x_all, w_qkv, units, a_own, w_out_own, layer, w_out_par):
    width = w_qkv.shape[0] // 3
    heads = width // HEAD
    rows, model = x_all.shape
    half = rows // 2 - small

    def body(refs):
        heads_into(refs, refs.meta, per, line, heads, half, small)
        for at, part in enumerate(chunks(rows)):
            made = nn(refs.a_own[part], refs.wo_own[...]) + nn(refs.a[part], refs.wo_par[...])
            getattr(refs, f"mine{at}")[...] = made.astype(bf16)

    operands = dict(
        meta=(SCALAR, meta),
        low=(FAR, x_all),
        w_qkv=(FAR, w_qkv),
        units=(FAR, units),
        a_own=(FAR, a_own),
        wo_own=(FAR, w_out_own, layer),
        wo_par=(FAR, w_out_par),
    )
    return run("attend", body, operands, heads_results(rows, width) | parts_out(rows, model))


def ffn_into(refs, line):
    bias = refs.units[line : line + 1]
    rows_all = refs.hidden.held.shape[0]
    for rows in chunks(rows_all):
        hidden, slope = gelu_pair(nn(refs.low[rows], refs.w_up[...]) + bias)
        refs.hidden[rows] = hidden.astype(bf16)
        refs.slope[rows] = slope.astype(bf16)
        if rows.stop * 2 % rows_all == 0:
            refs.hidden.flush(rows.stop * 2 // rows_all - 1)
            refs.slope.flush(rows.stop * 2 // rows_all - 1)


def hidden_results(rows, units):
    made = ([(0, rows // 2), (rows // 2, rows)], (rows, units), bf16)
    return dict(hidden=made, slope=made)


def ffn_first(meta, line, norm, w_up, layer, units):
    rows, model = norm.base.shape

    def body(refs):
        norm_into(refs, norm.line)
        ffn_into(refs, line)

    operands = dict(meta=(SCALAR, meta)) | parts_in(norm)
    operands |= dict(
        base=(FAR, norm.base), vecs=(FAR, norm.vecs), w_up=(FAR, w_up, layer), units=(FAR, units)
    )
    return run("ffn", body, operands, norm_results(rows, model) | hidden_results(rows, w_up.shape[2]))


def ffn_second(meta, line, y_low, w_up, units, hidden_own, w_down_own, layer, w_down_par):
    rows, model = y_low.shape

    def body(refs):
        ffn_into(refs, line)
        for at, part in enumerate(chunks(rows)):
            made = nn(refs.hidden_own[part], refs.wd_own[...]) + nn(refs.hidden[part], refs.wd_par[...])
            getattr(refs, f"mine{at}")[...] = made.astype(bf16)

    operands = dict(
        meta=(SCALAR, meta),
        low=(FAR, y_low),
        w_up=w_up,
        units=(FAR, units),
        hidden_own=(FAR, hidden_own),
        wd_own=(FAR, w_down_own, layer),
        wd_par=w_down_par,
    )
    results = hidden_results(rows, w_up[1].shape[-1]) | parts_out(rows, model)
    return run("ffn", body, operands, results)


def norm_back_results(rows, width):
    return dict(
        g=(FAR, (rows, width), f32), low=(FAR, (rows, width), bf16), sums=(FAR, (8, width), f32)
    )


def ffn_back(meta, norm, kept, y_low, w_up, w_down, extra, other):
    rows, model = y_low.shape
    units = w_up[1].shape[-1]
    count = units + model + (0 if extra is None else extra.shape[0])
    first = norm is not None
    operands = dict(meta=(SCALAR, meta))
    operands |= norm.operands if first else dict(low=(FAR, other.low))
    operands |= dict(w_down=w_down, slope=(FAR, kept.slope), hidden=(FAR, kept.hidden), y=(FAR, y_low))
    if extra is not None:
        operands |= dict(extra=(FAR, extra))
    results = dict(
        grads=([(0, units), (units, count)], (count, model), bf16), line=(FAR, (8, units), f32)
    )
    if first:
        results |= norm_back_results(rows, model) | dict(pre=(FAR, (rows, units), bf16))
    else:
        operands |= dict(w_up=w_up, pre_other=(FAR, other.pre), w_up_other=other.w_up)
        results |= parts_out(rows, model)

    def body(refs):
        if first:
            norm_back_into(refs, norm.line)
            pre_ref = refs.pre
        else:
            pre_ref = refs.scratch[0]
        total = None
        for at in chunks(rows):
            pre = (refs.slope[at].astype(f32) * nt(refs.low[at], refs.w_down[...])).astype(bf16)
            pre_ref[at] = pre
            line = jnp.sum(pre.astype(f32), 0, keepdims=True)
            total = line if total is None else total + line
        if first:
            pre_ref.flush()
        refs.line[0:1] = total
        refs.line[1:] = jnp.zeros((7, units), f32)
        refs.line.flush()
        refs.grads[:units] = tn(refs.hidden[...], refs.low[...]).astype(bf16)
        refs.grads.flush(0)
        refs.grads[units : units + model] = tn(refs.y[...], pre_ref[...]).astype(bf16)
        if extra is not None:
            refs.grads[units + model :] = refs.extra[...]
        refs.grads.flush(1)
        if not first:
            for at, part in enumerate(chunks(rows)):
                made = nt(pre_ref[part], refs.w_up[...]) + nt(refs.pre_other[part], refs.w_up_other[...])
                getattr(refs, f"mine{at}")[...] = made.astype(bf16)

    scratch = () if first else (pltpu.VMEM((rows, units), bf16),)
    return run("ffn_back", body, operands, results, scratch=scratch)


def attend_back(meta, per, small, norm, kept, x_all, w_qkv, w_out, other, last):
    rows, model = x_all.shape
    width = w_out[1].shape[-2]
    half = rows // 2 - small
    first = norm is not None
    scale = HEAD**-0.5
    operands = dict(meta=(SCALAR, meta))
    operands |= norm.operands if first else dict(low=(FAR, other.low))
    operands |= dict(
        w_out=w_out,
        a=(FAR, kept.a),
        k=(FAR, kept.k),
        q=(FAR, kept.q),
        lse=(FAR, kept.lse),
        v=(FAR, kept.v),
        x=(FAR, x_all),
    )
    results = dict(
        grads=([(0, 3 * width), (3 * width, 4 * width)], (4 * width, model), bf16),
        line=(FAR, (8, 3 * width), f32),
    )
    if first:
        results |= norm_back_results(rows, model) | dict(g_qkv=(FAR, (rows, 3 * width), bf16))
    else:
        operands |= dict(w_qkv=w_qkv, g_other=(FAR, other.g_qkv), w_other=(FAR, other.w_qkv))
        if last:
            operands |= dict(g_norm=(FAR, other.g))
            results |= dict(own=(NEAR, (rows // 2, model), f32), away=(NEAR, (rows // 2, model), bf16))
        else:
            results |= parts_out(rows, model)
    scratch = [
        pltpu.VMEM((rows, width), bf16),
        pltpu.VMEM((2 * half, HEAD), f32),
        pltpu.VMEM((2 * half, HEAD), f32),
    ]
    if not first:
        scratch.append(pltpu.VMEM((rows, 3 * width), bf16))

    def body(refs):
        if first:
            norm_back_into(refs, norm.line)
            g_ref = refs.g_qkv
        else:
            g_ref = refs.scratch[3]
        da_ref, dv_sum, dk_sum = refs.scratch[:3]
        low = refs.low[...]
        da_ref[...] = nt(low, refs.w_out[...]).astype(bf16)
        refs.grads[3 * width :] = tn(refs.a[...], low).astype(bf16)
        refs.grads.flush(1)
        same = small_same(refs.meta, per, small)
        ones = jnp.ones((8, HEAD), f32)
        for head in range(width // HEAD):
            cols = slice(head * HEAD, (head + 1) * HEAD)
            line = slice(head, head + 1)
            k_head = refs.k[:, cols]
            v_head = refs.v[:, cols]
            q_head = refs.q[:, cols] * scale
            da_head = da_ref[:, cols]
            inner = da_head.astype(f32) * refs.a[:, cols].astype(f32)
            delta = exact(ones, inner, ((1,), (1,)))[0:1]
            k_long = long_rows(k_head, half, small)
            v_long = long_rows(v_head, half, small)
            k_long_t = (k_long * scale).T
            for count, at in enumerate(q_starts(half, small, Q_ROWS)):
                here = slice(at, at + Q_ROWS)
                q_blk = q_head[here]
                da_blk = da_head[here]
                probs = jnp.exp(nt(k_long, q_blk) - refs.lse[line, here])
                g_probs = nt(v_long, da_blk)
                g_scores = (probs * (g_probs - delta[:, here])).astype(bf16)
                g_v = nn(probs.astype(bf16), da_blk)
                g_k = nn(g_scores, q_blk)
                if count == 0:
                    dv_sum[...] = g_v
                    dk_sum[...] = g_k
                else:
                    dv_sum[...] += g_v
                    dk_sum[...] += g_k
                g_ref[here, cols] = nn(k_long_t, g_scores).T.astype(bf16)
            k_cols = slice(width + head * HEAD, width + (head + 1) * HEAD)
            v_cols = slice(2 * width + head * HEAD, 2 * width + (head + 1) * HEAD)
            for part, base in enumerate((0, half + small)):
                g_ref[base : base + half, k_cols] = dk_sum[part * half : (part + 1) * half].astype(bf16)
                g_ref[base : base + half, v_cols] = dv_sum[part * half : (part + 1) * half].astype(bf16)
            k_small = small_rows(k_head, half, small)
            q_small = small_rows(q_head, half, small)
            da_small = small_rows(da_head, half, small)
            lse = jnp.concatenate(
                [refs.lse[line, half : half + small], refs.lse[line, 2 * half + small :]], 1
            )
            delta = jnp.concatenate([delta[:, half : half + small], delta[:, 2 * half + small :]], 1)
            probs = jnp.exp(jnp.where(same, nt(k_small, q_small), MASKED) - lse)
            g_probs = nt(small_rows(v_head, half, small), da_small)
            g_scores = (probs * (g_probs - delta)).astype(bf16)
            for where, made in (
                (cols, nn((k_small * scale).T, g_scores).T),
                (k_cols, nn(g_scores, q_small)),
                (v_cols, nn(probs.astype(bf16), da_small)),
            ):
                g_ref[half : half + small, where] = made[:small].astype(bf16)
                g_ref[2 * half + small :, where] = made[small:].astype(bf16)
        if first:
            g_ref.flush()
        g_all = g_ref[...]
        refs.grads[: 3 * width] = tn(g_all, refs.x[...]).astype(bf16)
        refs.grads.flush(0)
        refs.line[0:1] = jnp.sum(g_all.astype(f32), 0, keepdims=True)
        refs.line[1:] = jnp.zeros((7, 3 * width), f32)
        refs.line.flush()
        if not first:
            made = nn(g_all, refs.w_qkv[...]) + nn(refs.g_other[...], refs.w_other[...])
            if last:
                own = rows // 2
                made = made + jnp.concatenate([refs.g_norm[:own], jnp.zeros((own, model), f32)], 0)
                high = made.astype(bf16)
                rest = (made - high.astype(f32)).astype(bf16)
                core = facts(refs.meta, per)[0]
                place = row_places(refs.meta, per, half, small, 1)
                at = lax.broadcasted_iota(i32, (own, rows), 0)
                pick = (place == core * own + at).astype(bf16)
                refs.own[...] = nn(pick, high) + nn(pick, rest)
                refs.away[...] = nn((place == (1 - core) * own + at).astype(bf16), high).astype(bf16)
            else:
                for at, part in enumerate(chunks(rows)):
                    getattr(refs, f"mine{at}")[...] = made[part].astype(bf16)

    return run("attend_back", body, operands, results, scratch=scratch)


def halve(place, value, other):
    rows, width = value.shape[0] // 2, value.shape[1]
    kind = value.dtype
    if rows % 16:

        def take(which):
            return sum(
                lax.dynamic_slice_in_dim(part, which * rows, rows, 0).astype(f32) for part in (value, other)
            ).astype(kind)

        return take(place[0]), take(1 - place[0])

    def body(refs):
        place = refs.place[0]
        for out, which in ((refs.sent, 1 - place), (refs.kept, place)):
            part = pl.ds(pl.multiple_of(which * rows, 16), rows)
            out[...] = (refs.value[part].astype(f32) + refs.other[part].astype(f32)).astype(kind)

    made = (NEAR, (rows, width), kind)
    got = run(
        "halve",
        body,
        dict(place=(SCALAR, place), value=(NEAR, value), other=(NEAR, other)),
        dict(kept=made, sent=made),
    )
    return got.kept, got.sent


def join(place, mine, other):
    rows, width = mine.shape
    if rows % 16:
        return jnp.where(place[0] == 1, jnp.concatenate([other, mine], 0), jnp.concatenate([mine, other], 0))

    def body(refs):
        place = refs.place[0]
        refs.out[pl.ds(pl.multiple_of(place * rows, 16), rows)] = refs.mine[...]
        refs.out[pl.ds(pl.multiple_of((1 - place) * rows, 16), rows)] = refs.other[...]

    return run(
        "join",
        body,
        dict(place=(SCALAR, place), mine=(NEAR, mine), other=(NEAR, other)),
        dict(out=(NEAR, (2 * rows, width), mine.dtype)),
    ).out


def slices(meta, weights, strips, strip_rows):
    given = [*weights, *strips]
    model = given[-1][0].shape[2]

    def body(meta_ref, *refs):
        sems, outs = refs[-1], refs[len(given) : -1]
        copies = []
        for at, (_, layer) in enumerate(given):
            if at < len(weights):
                copies.append((refs[at].at[layer], outs[at]))
            else:
                rows = pl.ds(pl.multiple_of(meta_ref[0] * strip_rows, 16), strip_rows)
                part = pl.ds((at - len(weights)) * strip_rows, strip_rows)
                copies.append((refs[at].at[layer, rows], outs[-1].at[part]))
        copies = [pltpu.make_async_copy(*pair, sems.at[at]) for at, pair in enumerate(copies)]
        for copy in copies:
            copy.start()
        for copy in copies:
            copy.wait()

    made = [pltpu.VMEM(array.shape[1:], array.dtype) for array, _ in weights]
    made += [pltpu.VMEM((len(strips) * strip_rows, model), bf16)] if strips else []
    return pl.pallas_call(
        body,
        out_shape=tuple(made),
        in_specs=[SMEM] + [HBM] * len(given),
        out_specs=(VMEM,) * len(made),
        scratch_shapes=[pltpu.SemaphoreType.DMA((len(given),))],
        cost_estimate=pl.CostEstimate(flops=COST, transcendentals=0, bytes_accessed=0),
        name="slices",
    )(meta, *[pltpu.with_memory_space_constraint(array, pltpu.HBM) for array, _ in given])


def gather_small(meta, per, b_out, b_down, ln_gain, ln_shift, b_up, b_qv, queries):
    layers, units = b_up.shape
    model = b_out.shape[1]
    width = b_qv.shape[2]
    q_group, q_piece, dim = queries.shape
    q_rows = q_group * q_piece

    def body(meta, bo_ref, bd_ref, gain_ref, shift_ref, bu_ref, bqv_ref, q_ref, vec_out, line_out, carried_out):
        vec_out[...] = jnp.zeros(vec_out.shape, f32)
        line_out[...] = jnp.zeros(line_out.shape, f32)
        for layer in range(layers):
            for at, ref in ((0, bo_ref), (1, bd_ref)):
                first = 8 * (2 * layer + at)
                vec_out[first : first + 1] = ref[layer : layer + 1]
                vec_out[first + 1 : first + 2] = gain_ref[layer, at : at + 1]
                vec_out[first + 2 : first + 3] = shift_ref[layer, at : at + 1]
                line_out[2 * layer + 1 : 2 * layer + 2, at * width : (at + 1) * width] = bqv_ref[
                    layer, at : at + 1
                ]
            line_out[2 * layer : 2 * layer + 1] = bu_ref[layer : layer + 1].astype(f32)
        for at in range(q_group):
            carried_out[at * q_piece : (at + 1) * q_piece] = q_ref[at]
        lane = lax.broadcasted_iota(i32, (CARRIED - q_rows, dim), 1)
        row = lax.broadcasted_iota(i32, (CARRIED - q_rows, dim), 0)
        made = jnp.zeros((CARRIED - q_rows, dim), f32)
        for at in range(2 * per):
            made = jnp.where((lane == at) & (row == 0), meta[2 + 2 * per + at].astype(f32), made)
        carried_out[q_rows:] = made.astype(bf16)

    return pl.pallas_call(
        body,
        out_shape=(
            jax.ShapeDtypeStruct((16 * layers, model), f32),
            jax.ShapeDtypeStruct((-(-2 * layers // 8) * 8, units), f32),
            jax.ShapeDtypeStruct((CARRIED, dim), bf16),
        ),
        in_specs=[SMEM] + [VMEM] * 7,
        out_specs=(VMEM,) * 3,
        cost_estimate=pl.CostEstimate(flops=COST, transcendentals=0, bytes_accessed=0),
        name="gather_small",
    )(meta, b_out, b_down, ln_gain, ln_shift, b_up, b_qv, queries)


def turn(meta, per, small, x_own, x_other):
    own, model = x_own.shape
    rows = 2 * own

    def body(refs):
        core = facts(refs.meta, per)[0]
        place = row_places(refs.meta, per, own - small, small, 0)
        at = lax.broadcasted_iota(i32, (rows, own), 1)
        made = nn((place == core * own + at).astype(bf16), refs.mine[...])
        made = made + nn((place == (1 - core) * own + at).astype(bf16), refs.came[...])
        made = made.astype(bf16)
        refs.near[...] = made
        refs.low[...] = made
        refs.low.flush()

    operands = dict(meta=(SCALAR, meta), mine=(NEAR, x_own), came=(NEAR, x_other))
    results = dict(near=(NEAR, (rows, model), bf16), low=(FAR, (rows, model), bf16))
    return run("turn", body, operands, results)


CARRIED = 32


def query_of(at, q_group, q_piece):
    return at // q_piece % q_group


def score(meta, per, small, norm, w_proj, carried, q_group, q_piece, n_mp):
    rows, model = norm.base.shape
    half = rows // 2 - small
    dim = w_proj.shape[1]
    q_rows = q_group * q_piece
    q_tok = q_rows * n_mp
    count = per * q_tok
    n_dp = carried.shape[0] // (n_mp * CARRIED)

    def body(refs):
        norm_into(refs, norm.line)
        groups = facts(refs.meta, per)[4]
        for at in range(per):
            for piece in range(n_mp):
                side = piece % 2 * 2 + piece // 2
                source = pl.multiple_of((side * n_dp + groups[at]) * CARRIED, CARRIED)
                first = at * q_tok + piece * q_rows
                refs.flat_q[first : first + q_rows] = refs.carried[pl.ds(source, q_rows)]
        emb = nn(refs.low[...], refs.w_proj[...])
        unit = emb * lax.rsqrt(jnp.sum(emb * emb, -1, keepdims=True) + UNIT_EPS)
        segment = row_segments(refs.meta, per, half, small)
        owner = lax.broadcasted_iota(i32, (rows, count), 1) // q_tok == segment
        similar = nt(unit.astype(bf16), refs.flat_q[...])
        terms = jnp.where(owner, jnp.exp(SHARP * (similar - 1.0)), 0.0)
        totals = jnp.sum(terms, 0, keepdims=True)
        refs.totals[...] = jnp.broadcast_to(totals, (8, count))
        _, micro, _, _, _ = facts(refs.meta, per)
        slot = (refs.meta[0] * 2 + micro) * per
        lane = lax.broadcasted_iota(i32, (8, count), 1)
        length = jnp.zeros((8, count), f32)
        for at in range(per):
            size = jnp.full((8, count), refs.meta[2 + micro * per + at].astype(f32))
            length = jnp.where(lane // q_tok == at, size, length)
        term = (jnp.log(jnp.broadcast_to(totals, (8, count))) - jnp.log(length)) / SHARP + 1.0
        row = lax.broadcasted_iota(i32, (8, count), 0)
        term = jnp.where(query_of(lane, q_group, q_piece) == row, term, 0.0)
        n_pass = refs.logits.shape[1]
        target = lax.broadcasted_iota(i32, (count, n_pass), 1)
        source = lax.broadcasted_iota(i32, (count, n_pass), 0)
        pick = (source // q_tok + slot == target).astype(f32)
        refs.logits[...] = exact(term, pick) / TEMPER

    n_pass = carried.shape[0] // (n_mp * CARRIED) * 2 * per
    operands = dict(meta=(SCALAR, meta)) | parts_in(norm)
    operands |= dict(
        base=(FAR, norm.base),
        vecs=(FAR, norm.vecs),
        carried=(NEAR, carried),
        w_proj=(FAR, w_proj),
    )
    results = norm_results(rows, model, keep=False) | dict(
        flat_q=(NEAR, (count, dim), bf16),
        totals=(NEAR, (8, count), f32),
        logits=(NEAR, (8, n_pass), f32),
    )
    return run("score", body, operands, results)


def loss_back(meta, per, small, logits, groups, targets, totals, flat_q, final, w_proj, q_group, q_piece, n_mp):
    n_dp, n_pass = targets.shape[1], logits.shape[1]
    rows, model = final.shape
    half = rows // 2 - small
    dim = w_proj.shape[1]
    q_rows = q_group * q_piece
    q_tok = q_rows * n_mp
    count = per * q_tok
    held = n_dp * q_rows * (n_mp // 2)

    def body(refs):
        meta = refs.meta
        core, micro, _, _, own_groups = facts(meta, per)
        member = refs.groups[...] == lax.broadcasted_iota(i32, (n_dp, n_pass), 0)
        lane = lax.broadcasted_iota(i32, (n_dp, n_pass), 1)
        g_rows = []
        for query in range(q_group):
            logit = refs.logits[query : query + 1]
            spread = jnp.where(member, logit, FLOOR)
            top = jnp.max(spread, 1, keepdims=True)
            mass = jnp.sum(jnp.where(member, jnp.exp(spread - top), 0.0), 1, keepdims=True)
            lse = top + jnp.log(mass)
            hit = lane == refs.targets[query]
            refs.loss[query] = lse - jnp.sum(jnp.where(hit, logit, 0.0), 1, keepdims=True)
            lse_pass = jnp.sum(jnp.where(member, lse, 0.0), 0, keepdims=True)
            hits = jnp.sum(jnp.where(hit & member, 1.0, 0.0), 0, keepdims=True)
            g_rows.append(jnp.exp(logit - lse_pass) - hits)
        g_logit = jnp.concatenate(g_rows + [jnp.zeros((8 - q_group, n_pass), f32)], 0)
        slot = (meta[0] * 2 + micro) * per
        lane = lax.broadcasted_iota(i32, (n_pass, count), 0)
        at = lax.broadcasted_iota(i32, (n_pass, count), 1)
        wide = exact(g_logit, (at // q_tok + slot == lane).astype(f32))
        at = lax.broadcasted_iota(i32, (8, count), 1)
        row = lax.broadcasted_iota(i32, (8, count), 0)
        wide = jnp.where(query_of(at, q_group, q_piece) == row, wide, 0.0)
        wide = jnp.sum(wide, 0, keepdims=True)
        g_total = (wide / TEMPER) / (SHARP * refs.totals[0:1])
        low = refs.final[...]
        emb = nn(low, refs.w_proj[...])
        scale = lax.rsqrt(jnp.sum(emb * emb, -1, keepdims=True) + UNIT_EPS)
        unit = emb * scale
        unit_low = unit.astype(bf16)
        segment = row_segments(meta, per, half, small)
        owner = lax.broadcasted_iota(i32, (rows, count), 1) // q_tok == segment
        similar = nt(unit_low, refs.flat_q[...])
        terms = jnp.where(owner, jnp.exp(SHARP * (similar - 1.0)), 0.0)
        g_sim = (SHARP * terms * g_total).astype(bf16)
        g_unit = nn(g_sim, refs.flat_q[...])
        g_emb = scale * (g_unit - unit * jnp.sum(g_unit * unit, -1, keepdims=True))
        g_emb = g_emb.astype(bf16)
        refs.grad[...] = nt(g_emb, refs.w_proj[...])
        refs.proj[...] = tn(g_emb, low).astype(bf16)
        g_picked = tn(g_sim, unit_low)
        row = lax.broadcasted_iota(i32, (held, count), 0)
        source = lax.broadcasted_iota(i32, (held, count), 1)
        group = row // q_rows % n_dp
        piece = row // (q_rows * n_dp) * 2 + core
        want = piece * q_rows + row % q_rows
        line = lax.broadcasted_iota(i32, (1, count), 1) // q_tok
        source_group = jnp.zeros((1, count), i32)
        for passage in range(per):
            source_group = jnp.where(line == passage, own_groups[passage], source_group)
        pick = ((source % q_tok == want) & (source_group == group)).astype(f32)
        refs.queries[...] = exact(pick, g_picked)

    operands = dict(
        meta=(SCALAR, meta),
        logits=(NEAR, logits),
        groups=(NEAR, groups),
        targets=(NEAR, targets),
        totals=(NEAR, totals),
        flat_q=(NEAR, flat_q),
        final=(FAR, final),
        w_proj=(FAR, w_proj),
    )
    results = dict(
        loss=(NEAR, (q_group, n_dp, 1), f32),
        queries=(NEAR, (held, dim), f32),
        proj=(NEAR, (dim, model), bf16),
        grad=(NEAR, (rows, model), f32),
    )
    return run("loss_back", body, operands, results)


def pack(meta, sums, own, par):
    model = sums[0].shape[1]
    first = 8 * len(sums)
    rows = first + -(-2 * len(own) // 8) * 8
    operands = dict(meta=(SCALAR, meta)) | {f"sum{at}": (FAR, value) for at, value in enumerate(sums)}
    for layer, pairs in enumerate(zip(own, par)):
        for side, pair in enumerate(pairs):
            for at, value in enumerate(pair):
                operands[f"line{layer}{side}{at}"] = (FAR, value)

    def body(refs):
        for side, out in enumerate((refs.own, refs.par)):
            out[first:] = jnp.zeros((rows - first, model), f32)
            for at in range(len(sums)):
                out[8 * at : 8 * at + 8] = getattr(refs, f"sum{at}")[...]
            for layer in range(len(own)):
                for at in range(2):
                    value = getattr(refs, f"line{layer}{side}{at}")
                    row = first + 2 * layer + at
                    out[row : row + 1, : value.held.shape[1]] = value[0:1]

    made = (NEAR, (rows, model), f32)
    got = run("pack", body, operands, dict(own=made, par=made))
    return got.own, got.par


def quarters(place, value, other):
    rows, width = value.shape[0] // 4, value.shape[1]

    def body(refs):
        for at in (1, 2, 3, 0):
            part = pl.ds(pl.multiple_of((refs.place[0] ^ at) * rows, 16), rows)
            made = refs.value[part].astype(f32) + refs.other[part].astype(f32)
            getattr(refs, f"part{at}")[...] = made.astype(value.dtype)

    operands = dict(place=(SCALAR, place), value=(NEAR, value), other=(NEAR, other))
    results = {f"part{at}": (NEAR, (rows, width), value.dtype) for at in range(4)}
    got = run("quarters", body, operands, results)
    return [getattr(got, f"part{at}") for at in range(4)]


def join_quarters(place, *parts):
    rows, width = parts[0].shape

    def body(refs):
        for at in range(4):
            part = pl.ds(pl.multiple_of((refs.place[0] ^ at) * rows, 16), rows)
            refs.out[part] = getattr(refs, f"part{at}")[...]

    operands = dict(place=(SCALAR, place)) | {f"part{at}": (NEAR, part) for at, part in enumerate(parts)}
    return run("join", body, operands, dict(out=(NEAR, (4 * rows, width), parts[0].dtype))).out


def add(*parts):
    def body(refs):
        total = sum(getattr(refs, f"part{at}")[...].astype(f32) for at in range(len(parts)))
        refs.out[...] = total.astype(parts[0].dtype)

    operands = {f"part{at}": (NEAR, part) for at, part in enumerate(parts)}
    return run("add", body, operands, dict(out=(NEAR, parts[0].shape, parts[0].dtype))).out


def on_device(
    passages_in,
    queries,
    w_qkv,
    b_qv,
    w_out,
    b_out,
    ln_gain,
    ln_shift,
    w_up,
    b_up,
    w_down,
    b_down,
    w_proj,
    lengths,
    passage_group,
    positive,
):
    n_mp = lax.axis_size("mp")
    n_dp = lax.axis_size("dp")
    own, model = passages_in.shape
    micro_count, per = lengths.shape
    tok_mb = own * n_mp // micro_count
    assert n_mp == 4 and micro_count == 2 and n_dp & (n_dp - 1) == 0
    layers = w_qkv.shape[0]
    width = w_qkv.shape[3]
    ff = w_up.shape[2]
    small = (tok_mb - LONGEST) // 2
    q_group, q_piece, dim = queries.shape
    q_rows = q_group * q_piece

    mp_here = lax.axis_index("mp")
    dp_here = lax.axis_index("dp")
    core, micro = mp_here % 2, mp_here // 2
    dp_bits = [1 << at for at in range(n_dp.bit_length() - 1)]

    def to_pair(value):
        return jax.tree.map(lambda part: lax.ppermute(part, "mp", [(at, at ^ 1) for at in range(n_mp)]), value)

    def to_x(value):
        return lax.ppermute(value, "mp", [(at, at ^ 2) for at in range(n_mp)])

    def to_dp(value, bit):
        return lax.ppermute(value, "dp", [(at, at ^ bit) for at in range(n_dp)])

    noted = []

    def here(value):
        return lax.optimization_barrier((value, noted[-1]))[0] if noted else value

    def note(value):
        noted.append(value)
        return value

    meta = jnp.concatenate(
        [jnp.stack([dp_here, mp_here]).astype(i32), lengths.reshape(-1), passage_group.reshape(-1)]
    )
    core_place, micro_place = core[None].astype(i32), micro[None].astype(i32)
    places = {bit: ((dp_here // bit) % 2)[None].astype(i32) for bit in dp_bits}

    w_qkv = w_qkv.transpose(0, 2, 3, 1).reshape(layers, 3 * width, model)
    x_other = to_pair(passages_in)
    strip_rows = model // n_dp

    def strips_of(meta, pairs):
        if strip_rows % 16 == 0:
            return slices(meta, [], pairs, strip_rows)[0]
        parts = [
            lax.dynamic_slice_in_dim(array[layer], dp_here * strip_rows, strip_rows, 0) for array, layer in pairs
        ]
        return jnp.concatenate(parts, 0)

    def gathered(strip):
        count = strip.shape[0] // strip_rows
        stack = lax.all_gather(strip, "dp", axis=0)
        if strip_rows % 16:
            parts = [stack[:, at * strip_rows : (at + 1) * strip_rows] for at in range(count)]
            return [(FAR, part.reshape(-1, model)) for part in parts]
        return [
            (FAR, stack, (slice(None), slice(at * strip_rows, (at + 1) * strip_rows))) for at in range(count)
        ]

    def after(value, first):
        return lax.optimization_barrier((value, first))[0]

    strip = strips_of(meta, [(w_up, 0)])
    strip_par = to_x(strip)
    vecs, lines, first_carried = gather_small(
        after(meta, strip), per, b_out, b_down, ln_gain, ln_shift, b_up, b_qv, queries
    )
    sent = slices(after(meta, lines), [(w_qkv, 0), (w_out, 0), (w_down, 0)], [], strip_rows)
    strip_par = after(strip_par, sent[0])
    w_par = [SimpleNamespace() for _ in range(layers)]
    (w_par[0].up,) = gathered(strip_par)
    w_par[0].qkv, w_par[0].out = (to_x(after(value, strip_par)) for value in sent[:2])
    lines_par = to_x(after(lines, strip_par))
    turned = turn(after(meta, sent[0]), per, small, passages_in, x_other)
    strips_par = [
        to_x(strips_of(after(meta, turned.low), [(w_up, layer), (w_down, layer)])) for layer in range(1, layers)
    ]

    def spread():
        value = first_carried
        steps = [((lambda v, bit=bit: to_dp(v, bit)), places[bit]) for bit in dp_bits]
        steps += [(to_x, micro_place), (to_pair, core_place)]
        for send, place in steps:
            other = send(value)
            yield
            value = note(join(here(place), value, other))
        yield value

    spreading, spread_out = spread(), []

    def spread_on():
        spread_out.append(next(spreading, None))

    spread_on()

    x_all, base, norm = turned.low, turned.low, None
    stored = []
    for layer in range(layers):
        par = w_par[layer]
        att_own = attend_first(
            here(meta), per, small, 2 * layer + 1, turned.near if norm is None else None, norm, w_qkv, layer, lines
        )
        note(att_own.lse)
        if layer == 0:
            spread_on()
        if norm is not None:
            x_all, base = att_own.low, att_own.y
        att_par = attend_second(
            here(meta), per, small, 2 * layer + 1, x_all, par.qkv, lines_par, att_own.a, w_out, layer, par.out
        )
        note(att_par.lse)
        if layer == 0:
            strips_par = [here(strip) for strip in strips_par]
            w_par[0].down = (FAR, to_x(after(sent[2], strips_par[0])))
            for at in range(1, layers):
                w_par[at].up, w_par[at].down = gathered(strips_par[at - 1])
        norm = SimpleNamespace(
            mine=parts_of(att_par), came=to_pair(parts_of(att_par)), base=base, vecs=vecs, line=2 * layer
        )
        spread_on()
        ffn_own = ffn_first(here(meta), 2 * layer, norm, w_up, layer, lines)
        note(ffn_own.r)
        if layer != 0:
            spread_on()
        if layer + 1 < layers:
            at = layer + 1
            pieces = slices(here(meta), [(w_qkv, at), (w_out, at)], [], strip_rows)
            w_par[at].qkv, w_par[at].out = (to_x(value) for value in pieces)
        ffn_par = ffn_second(
            here(meta), 2 * layer, ffn_own.low, par.up, lines_par, ffn_own.hidden, w_down, layer, par.down
        )
        note(ffn_par.mine0)
        norm = SimpleNamespace(
            mine=parts_of(ffn_par),
            came=to_pair(parts_of(ffn_par)),
            base=ffn_own.y,
            vecs=vecs,
            line=2 * layer + 1,
        )
        if layer == 0:
            spread_on()
        stored.append([x_all, att_own, att_par, ffn_own, ffn_par])
    spread_out += list(spreading)
    carried = next(value for value in spread_out if value is not None)
    groups = carried.reshape(n_mp, n_dp, CARRIED, dim)[0, :, q_rows, : passage_group.size]
    groups = groups.reshape(1, -1).astype(i32)

    found = score(here(meta), per, small, norm, w_proj, carried, q_group, q_piece, n_mp)
    norms_after = [stored[layer][1] for layer in range(1, layers)] + [found]
    logits = found.logits
    logits = logits + to_x(logits)
    for bit in dp_bits:
        logits = logits + to_dp(logits, bit)
    back = loss_back(
        meta,
        per,
        small,
        logits,
        groups,
        positive.reshape(n_dp, q_group).T[:, :, None],
        found.totals,
        found.flat_q,
        found.low,
        w_proj,
        q_group,
        q_piece,
        n_mp,
    )
    note(back.grad)
    query_loss = lax.dynamic_index_in_dim(back.loss[:, :, 0], dp_here, 1, keepdims=False)

    def total(theirs):
        other = to_x(here(theirs))
        value = yield
        yield
        for bit in dp_bits:
            value, sent = halve(here(places[bit]), value, other)
            note(value)
            other = to_dp(sent, bit)
            yield
        value = note(add(here(value), other))
        for bit in reversed(dp_bits):
            other = to_dp(value, bit)
            yield
            value = note(join(here(places[bit]), value, other))
        yield value

    def total_early(theirs):
        other = to_x(here(theirs))
        value = yield
        yield
        value, sent = halve(here(places[1]), value, other)
        note(value)
        other = to_dp(sent, 1)
        yield
        value = note(add(here(value), other))
        value = lax.psum(value, "dp", axis_index_groups=[list(range(side, n_dp, 2)) for side in range(2)])
        yield
        value = here(value)
        other = to_dp(value, 1)
        yield
        yield note(join(here(places[1]), value, other))

    def query_sums():
        value = back.queries
        rows = value.shape[0] // 2
        other = to_x(lax.dynamic_slice_in_dim(value, (1 - micro) * rows, rows, 0))
        value = lax.dynamic_slice_in_dim(value, micro * rows, rows, 0)
        for bit in reversed(dp_bits):
            yield
            value, sent = halve(here(places[bit]), value, other)
            note(value)
            other = to_dp(sent, bit)
        yield
        yield value + other

    queried = query_sums()
    next(queried)
    running = []

    def advance(which, count=1):
        for _ in range(count):
            got = next(running[which])
        return got

    finals = [None] * (2 * layers)
    rep_sums, own_sums, par_sums = [None] * (2 * layers), [None] * layers, [None] * layers
    grads = dict(grad=(NEAR, back.grad))
    for layer in reversed(range(layers)):
        x_all, att_own, att_par, ffn_own, ffn_par = stored[layer]
        par = w_par[layer]
        last = layer == layers - 1
        extra = back.proj if last else None

        def way(line, kept):
            rest = dict(n=(FAR, kept.n), r=(FAR, kept.r), vecs=(FAR, vecs))
            return SimpleNamespace(operands=grads | rest, line=line)

        got_par = ffn_back(
            here(meta),
            way(2 * layer + 1, norms_after[layer]),
            ffn_par,
            ffn_own.low,
            par.up,
            par.down,
            extra,
            None,
        )
        note(got_par.line)
        if last:
            next(queried)
        else:
            advance(1)
        running.append((total_early if last else total)(got_par.grads))
        advance(-1)
        other = SimpleNamespace(low=got_par.low, pre=got_par.pre, w_up=par.up)
        got_own = ffn_back(
            here(meta), None, ffn_own, ffn_own.low, (FAR, w_up, layer), (FAR, w_down, layer), extra, other
        )
        note(got_own.line)
        running[-1].send(got_own.grads)
        rep_sums[2 * layer + 1] = got_par.sums
        bup = (got_own.line, got_par.line)
        exchanged = SimpleNamespace(mine=parts_of(got_own), came=to_pair(parts_of(got_own)))
        grads = parts_in(exchanged) | dict(base=(FAR, got_par.g))
        if last:
            next(queried)
        else:
            advance(0)
        got_par = attend_back(
            here(meta),
            per,
            small,
            way(2 * layer, ffn_own),
            att_par,
            x_all,
            (FAR, par.qkv),
            (FAR, par.out),
            None,
            False,
        )
        note(got_par.line)
        if not last:
            advance(2)
            advance(1)
        running.append(total(got_par.grads))
        advance(-1)
        if last:
            next(queried)
        other = SimpleNamespace(low=got_par.low, g_qkv=got_par.g_qkv, w_qkv=par.qkv, g=got_par.g)
        got_own = attend_back(
            here(meta), per, small, None, att_own, x_all, (FAR, w_qkv, layer), (FAR, w_out, layer), other, layer == 0
        )
        note(got_own.line)
        running[-1].send(got_own.grads)
        rep_sums[2 * layer] = got_par.sums
        own_sums[layer] = (bup[0], got_own.line)
        par_sums[layer] = (bup[1], got_par.line)
        if layer:
            exchanged = SimpleNamespace(mine=parts_of(got_own), came=to_pair(parts_of(got_own)))
            grads = parts_in(exchanged) | dict(base=(FAR, got_par.g))
        if last:
            advance(0)
            query_grad = [value for value in queried if value is not None][0].reshape(q_group, q_piece, dim)
    input_grad = got_own.own + to_pair(got_own.away).astype(f32)

    count = 2 * layers * 8
    flat, flat_par = pack(here(meta), rep_sums, own_sums, par_sums)
    flat_other = to_x(flat_par)

    def flat_sums():
        value, other = flat, flat_other
        for bit in dp_bits:
            yield
            value = note(add(here(value), other))
            other = to_dp(value, bit)
        yield
        yield note(add(here(value), other))

    running.append(flat_sums())
    advance(-1)
    finals = [None] * len(running)
    turns = TURNS if n_dp == 8 and layers == 2 else []
    for which in turns:
        finals[which] = advance(which)
    for which in range(len(running)):
        for got in running[which]:
            finals[which] = got
    flat = finals.pop()
    lists = [[], [], [], []]
    for layer in range(layers):
        summed = finals[2 * (layers - 1 - layer)]
        lists[3].append(summed[:ff])
        lists[2].append(summed[ff : ff + model])
        if layer == layers - 1:
            g_wproj = summed[ff + model :].astype(f32).T
        summed = finals[2 * (layers - 1 - layer) + 1]
        lists[0].append(summed[: 3 * width])
        lists[1].append(summed[3 * width :])
    norms = flat[:count].reshape(layers, 2, 8, model)
    units = flat[count : count + 2 * layers].reshape(layers, 2, model)
    g_bqv = jnp.stack([units[:, 1, :width], units[:, 1, 2 * width : 3 * width]], 1)
    g_wqkv, g_wout, g_wup, g_wdown = (
        jnp.stack([value.astype(f32) for value in values]) for values in lists
    )
    g_wqkv = g_wqkv.reshape(layers, 3, width, model).transpose(0, 3, 1, 2)
    return (
        query_loss,
        input_grad,
        query_grad,
        g_wqkv,
        g_bqv,
        g_wout,
        norms[:, 0, 2],
        norms[:, :, 0],
        norms[:, :, 1],
        g_wup,
        units[:, 0],
        g_wdown,
        norms[:, 1, 2],
        g_wproj,
    )


def solution(mesh):
    placed = (
        P(("dp", "mp"), None),
        P("dp", "mp", None),
        P(None, None, None, "mp"),
        P(None, None, "mp"),
        P(None, "mp", None),
        P(),
        P(),
        P(),
        P(None, None, "mp"),
        P(None, "mp"),
        P(None, "mp", None),
        P(),
        P(),
        P("dp", None),
        P("dp", None),
        P(),
    )
    return jax.shard_map(
        on_device,
        mesh=mesh,
        in_specs=placed,
        out_specs=(
            P("dp"),
            P(("dp", "mp"), None),
            P("dp", "mp", None),
            P(None, None, None, "mp"),
            P(None, None, "mp"),
            P(None, "mp", None),
            P(),
            P(),
            P(),
            P(None, None, "mp"),
            P(None, "mp"),
            P(None, "mp", None),
            P(),
            P(),
        ),
        check_vma=False,
    )
```

```python
from types import SimpleNamespace

import jax
import jax.numpy as jnp
from jax import lax
from jax.experimental import pallas as pl
from jax.experimental.pallas import tpu as pltpu
from jax.sharding import PartitionSpec as P

HEAD = 64
LONGEST = 1024
SHARP = 4.0
TEMPER = 0.2
LN_EPS = 1e-12
UNIT_EPS = 1e-06
MASKED = -1000000000.0
FLOOR = -1e30
Q_ROWS = 512
AHEAD = 3
COST = 5000000
TURNS = (2, 3, 1, 4, 2, 3, 0, 1, 2, 4, 3, 1, 0, 2, 4, 3, 1, 2, 3, 4, 3, 2, 3)
VMEM_LIMIT = 40 * 2**20

bf16 = jnp.bfloat16
f32 = jnp.float32
i32 = jnp.int32
HIGH = lax.Precision.HIGHEST
VMEM = pl.BlockSpec(memory_space=pltpu.VMEM)
SMEM = pl.BlockSpec(memory_space=pltpu.SMEM)
HBM = pl.BlockSpec(memory_space=pltpu.HBM)
NEAR, FAR, SCALAR = range(3)


def nn(left_side, right_side):
    return lax.dot_general(
        left_side, right_side, (((1,), (0,)), ((), ())), preferred_element_type=f32
    )


def nt(left_side, right_side):
    return lax.dot_general(
        left_side, right_side, (((1,), (1,)), ((), ())), preferred_element_type=f32
    )


def tn(left_side, right_side):
    return lax.dot_general(
        left_side, right_side, (((0,), (0,)), ((), ())), preferred_element_type=f32
    )


def exact(left_side, right_side, dims=((1,), (0,))):
    return lax.dot_general(
        left_side, right_side, (dims, ((), ())), precision=HIGH, preferred_element_type=f32
    )


def gelu_pair(values):
    size = jnp.abs(values)
    t = 1.0 / (1.0 + (0.3275911 * 0.7071067811865476) * size)
    bell = jnp.exp(-0.5 * values * values)
    poly = t * (
        0.254829592
        + t * (-0.284496736 + t * (1.421413741 + t * (-1.453152027 + t * 1.061405429)))
    )
    tail = 0.5 * poly * bell
    phi = jnp.where(values < 0, tail, 1.0 - tail)
    return values * phi, phi + values * (0.3989422804014327 * bell)


class Fetched:
    def __init__(self, ref, part, held, sems, count, line):
        self.where = (ref, part, held, sems, count)
        self.held, self.line, self.due = held, line, True
        line.append(self)

    def copy(self):
        ref, part, held, sems, count = self.where
        return pltpu.make_async_copy(ref.at[part[0]] if part else ref, held, sems.at[count])

    def begin(self):
        self.line.remove(self)
        self.copy().start()

    def __getitem__(self, at):
        if self.due:
            if self in self.line:
                self.begin()
            if self.line:
                self.line[0].begin()
            self.copy().wait()
            self.due = False
        value = self.held[at]
        return value.reshape(-1, value.shape[-1]) if value.ndim == 3 else value


class Flushed:
    def __init__(self, ref, held, sems, pieces):
        self.ref, self.held, self.sems, self.pieces = ref, held, sems, pieces
        self.sent = []

    def __getitem__(self, at):
        return self.held[at]

    def __setitem__(self, at, value):
        self.held[at] = value

    def copy(self, which):
        first, last = self.pieces[which]
        rows = pl.ds(first, last - first)
        return pltpu.make_async_copy(self.held.at[rows], self.ref.at[rows], self.sems.at[which])

    def flush(self, which=0):
        self.copy(which).start()
        self.sent.append(which)


def stage(body):
    pl.when(lax.axis_index("dp") >= 0)(body)


def part_shape(shape, part=()):
    if isinstance(part, int):
        return shape[1:]
    return tuple(len(range(*at.indices(size))) for at, size in zip(part, shape)) + shape[len(part) :]


def run(name, body, operands, results, scratch=()):
    spaces = (pltpu.VMEM, pltpu.HBM)
    kinds = [given[0] for given in operands.values()]
    arrays = [
        given[1] if given[0] == SCALAR else pltpu.with_memory_space_constraint(given[1], spaces[given[0]])
        for given in operands.values()
    ]
    parts = [given[2:] for given in operands.values()]
    fetch = [at for at, kind in enumerate(kinds) if kind == FAR]
    made = list(results.values())
    pieces = {}
    for at, (kind, shape, _) in enumerate(made):
        if kind != NEAR:
            pieces[at] = [(0, shape[0])] if kind == FAR else kind
    added = [pltpu.VMEM(part_shape(arrays[at].shape, *parts[at]), arrays[at].dtype) for at in fetch]
    added += [pltpu.VMEM(made[at][1], made[at][2]) for at in pieces]
    added += [pltpu.SemaphoreType.DMA((max(len(fetch), 1),))]
    added += [pltpu.SemaphoreType.DMA((len(rows),)) for rows in pieces.values()]

    def outer(*refs):
        refs = list(refs)
        first = len(refs) - len(added)
        extra, refs = refs[first:], refs[:first]
        sems = extra[len(fetch) + len(pieces) :]
        line = []
        for count, at in enumerate(fetch):
            refs[at] = Fetched(refs[at], parts[at], extra[count], sems[0], count, line)
        for _ in range(min(AHEAD, len(line))):
            line[0].begin()
        outs = []
        for count, (at, rows) in enumerate(pieces.items()):
            out = Flushed(refs[len(operands) + at], extra[len(fetch) + count], sems[1 + count], rows)
            refs[len(operands) + at] = out
            outs.append(out)
        named = SimpleNamespace(scratch=refs[len(operands) + len(results) :])
        for key, ref in zip(list(operands) + list(results), refs):
            setattr(named, key, ref)
        body(named)
        for at in fetch:
            refs[at][0:1]
        for out in outs:
            for which in out.sent:
                out.copy(which).wait()

    given = pl.pallas_call(
        outer,
        out_shape=tuple(spaces[kind != NEAR](shape, dtype) for kind, shape, dtype in made),
        in_specs=[(VMEM, HBM, SMEM)[kind] for kind in kinds],
        out_specs=tuple(VMEM if kind == NEAR else HBM for kind, _, _ in made),
        scratch_shapes=list(scratch) + added,
        compiler_params=pltpu.CompilerParams(vmem_limit_bytes=VMEM_LIMIT),
        cost_estimate=pl.CostEstimate(flops=COST, transcendentals=0, bytes_accessed=0),
        name=name,
    )(*arrays)
    return SimpleNamespace(**dict(zip(results, given)))


def facts(meta, per):
    core, micro = meta[1] & 1, meta[1] >> 1
    ends, begin, last = [], 0, 0
    for at in range(per):
        length = meta[2 + micro * per + at]
        begin = begin + (length == LONGEST).astype(i32) * last
        last = last + length
        ends.append(last)
    groups = [meta[2 + 2 * per + micro * per + at] for at in range(per)]
    return core, micro, begin, ends, groups


def long_rows(values, half, small):
    return jnp.concatenate([values[0:half], values[half + small : 2 * half + small]], 0)


def small_rows(values, half, small):
    return jnp.concatenate([values[half : half + small], values[2 * half + small :]], 0)


def q_starts(half, small, step):
    return [at for base in (0, half + small) for at in range(base, base + half, step)]


def segment_of(place, ends):
    return sum((place >= end).astype(i32) for end in ends)


def small_same(meta, per, small):
    core, _, begin, ends, _ = facts(meta, per)

    def segments(shape, axis):
        at = lax.broadcasted_iota(i32, shape, axis)
        which = jnp.where(at < small, core, 1 - core)
        place = begin + LONGEST + which * small + jnp.where(at < small, at, at - small)
        total = LONGEST + 2 * small
        return segment_of(jnp.where(place >= total, place - total, place), ends)

    count = 2 * small
    return segments((count, count), 0) == segments((count, count), 1)


def row_places(meta, per, half, small, axis):
    core, _, begin, _, _ = facts(meta, per)
    own = half + small
    at = lax.broadcasted_iota(i32, (2 * own, 1) if axis == 0 else (1, 2 * own), axis)
    which = jnp.where(at < own, core, 1 - core)
    at = jnp.where(at < own, at, at - own)
    place = begin + jnp.where(at < half, which * half + at, LONGEST + which * small + at - half)
    total = LONGEST + 2 * small
    return jnp.where(place >= total, place - total, place)


def row_segments(meta, per, half, small):
    return segment_of(row_places(meta, per, half, small, 0), facts(meta, per)[3])


def chunks(rows):
    step = rows // PIECES
    return [slice(at, at + step) for at in range(0, rows, step)]


PIECES = 4


def both(refs, rows):
    at = rows.start // (rows.stop - rows.start)
    there = (at + PIECES // 2) % PIECES
    return getattr(refs, f"mine{at}")[...].astype(f32) + getattr(refs, f"came{there}")[...].astype(f32)


def parts_in(norm):
    made = {f"mine{at}": (NEAR, value) for at, value in enumerate(norm.mine)}
    return made | {f"came{at}": (NEAR, value) for at, value in enumerate(norm.came)}


def parts_out(rows, model):
    return {f"mine{at}": (NEAR, (rows // PIECES, model), bf16) for at in range(PIECES)}


def parts_of(got):
    return [getattr(got, f"mine{at}") for at in range(PIECES)]


def norm_into(refs, line):
    vecs = refs.vecs[8 * line : 8 * line + 8]
    for rows in chunks(refs.low.held.shape[0]):
        value = refs.base[rows].astype(f32) + (both(refs, rows) + vecs[0:1])
        centered = value - jnp.mean(value, -1, keepdims=True)
        inv_std = lax.rsqrt(jnp.mean(centered * centered, -1, keepdims=True) + LN_EPS)
        normed = centered * inv_std
        made = normed * vecs[1:2] + vecs[2:3]
        if hasattr(refs, "y"):
            refs.y[rows] = made
        refs.low[rows] = made.astype(bf16)
        refs.n[rows] = normed.astype(bf16)
        refs.r[rows] = inv_std
    for ref in (refs.low, refs.n, refs.r):
        ref.flush()
    if hasattr(refs, "y"):
        refs.y.flush()


def norm_results(rows, width, keep=True):
    made = dict(
        low=(FAR, (rows, width), bf16),
        n=(FAR, (rows, width), bf16),
        r=(FAR, (rows, 1), f32),
    )
    return made | (dict(y=(FAR, (rows, width), f32)) if keep else {})


def norm_back_into(refs, line):
    gain = refs.vecs[8 * line : 8 * line + 8][1:2]
    sums = None
    rows_all = refs.n.held.shape[0]
    for rows in chunks(rows_all):
        if hasattr(refs, "grad"):
            grad = refs.grad[rows]
        else:
            grad = refs.base[rows] + both(refs, rows)
        normed = refs.n[rows].astype(f32)
        inner = grad * gain
        made = refs.r[rows] * (
            inner
            - jnp.mean(inner, -1, keepdims=True)
            - normed * jnp.mean(inner * normed, -1, keepdims=True)
        )
        low = made.astype(bf16)
        refs.g[rows] = made
        refs.low[rows] = low
        lines = [
            jnp.sum(value, 0, keepdims=True) for value in (grad * normed, grad, low.astype(f32))
        ]
        sums = lines if sums is None else [a + b for a, b in zip(sums, lines)]
    refs.g.flush()
    refs.low.flush()
    for at, value in enumerate(sums):
        refs.sums[at : at + 1] = value
    refs.sums[3:] = jnp.zeros((5, sums[0].shape[1]), f32)
    refs.sums.flush()


def heads_into(refs, meta, per, line, heads, half, small):
    width = heads * HEAD

    bias = refs.units[line : line + 1]
    made = nt(refs.low[...], refs.w_qkv[...])
    refs.q[...] = (made[:, :width] + bias[:, :width]).astype(bf16)
    refs.k[...] = made[:, width : 2 * width].astype(bf16)
    refs.v[...] = (made[:, 2 * width :] + bias[:, width : 2 * width]).astype(bf16)
    for ref in (refs.q, refs.k, refs.v):
        ref.flush()
    scale = HEAD**-0.5
    same = small_same(meta, per, small)
    a_out, lse_out = refs.a, refs.lse
    for head in range(heads):
        cols = slice(head * HEAD, (head + 1) * HEAD)
        line = slice(head, head + 1)
        k_head = refs.k[:, cols]
        v_head = refs.v[:, cols]
        q_head = refs.q[:, cols] * scale
        k_long = long_rows(k_head, half, small)
        v_long_t = long_rows(v_head, half, small).T
        for at in q_starts(half, small, Q_ROWS):
            scores = nt(k_long, q_head[at : at + Q_ROWS])
            top = jnp.max(scores, 0, keepdims=True)
            probs = jnp.exp(scores - top)
            mass = jnp.sum(probs, 0, keepdims=True)
            out = nn(v_long_t, probs.astype(bf16)) / mass
            a_out[at : at + Q_ROWS, cols] = out.T.astype(bf16)
            lse_out[line, at : at + Q_ROWS] = top + jnp.log(mass)
        scores = nt(small_rows(k_head, half, small), small_rows(q_head, half, small))
        scores = jnp.where(same, scores, MASKED)
        top = jnp.max(scores, 0, keepdims=True)
        probs = jnp.exp(scores - top)
        mass = jnp.sum(probs, 0, keepdims=True)
        out = nn(small_rows(v_head, half, small).T, probs.astype(bf16)) / mass
        out = out.T.astype(bf16)
        a_out[half : half + small, cols] = out[:small]
        a_out[2 * half + small :, cols] = out[small:]
        lse = top + jnp.log(mass)
        lse_out[line, half : half + small] = lse[:, :small]
        lse_out[line, 2 * half + small :] = lse[:, small:]
    a_out.flush()
    lse_out.flush()


def heads_results(rows, width):
    made = (FAR, (rows, width), bf16)
    return dict(q=made, k=made, v=made, a=made, lse=(FAR, (8, rows), f32))


def attend_first(meta, per, small, line, x_all, norm, w_qkv, layer, units):
    width = w_qkv.shape[1] // 3
    heads = width // HEAD
    rows, model = (x_all if norm is None else norm.base).shape
    half = rows // 2 - small
    operands = dict(meta=(SCALAR, meta))
    results = {}
    if norm is None:
        operands |= dict(low=(NEAR, x_all))
    else:
        operands |= parts_in(norm) | dict(base=(FAR, norm.base), vecs=(FAR, norm.vecs))
        results = norm_results(rows, model)
    operands |= dict(w_qkv=(FAR, w_qkv, layer), units=(FAR, units))

    def body(refs):
        if norm is not None:
            norm_into(refs, norm.line)
        heads_into(refs, refs.meta, per, line, heads, half, small)

    return run("attend", body, operands, results | heads_results(rows, width))


def attend_second(meta, per, small, line, x_all, w_qkv, units, a_own, w_out_own, layer, w_out_par):
    width = w_qkv.shape[0] // 3
    heads = width // HEAD
    rows, model = x_all.shape
    half = rows // 2 - small

    def body(refs):
        heads_into(refs, refs.meta, per, line, heads, half, small)

        for at, part in enumerate(chunks(rows)):
            made = nn(refs.a_own[part], refs.wo_own[...]) + nn(refs.a[part], refs.wo_par[...])
            getattr(refs, f"mine{at}")[...] = made.astype(bf16)

    operands = dict(
        meta=(SCALAR, meta),
        low=(FAR, x_all),
        w_qkv=(FAR, w_qkv),
        units=(FAR, units),
        a_own=(FAR, a_own),
        wo_own=(FAR, w_out_own, layer),
        wo_par=(FAR, w_out_par),
    )
    return run("attend", body, operands, heads_results(rows, width) | parts_out(rows, model))


def ffn_into(refs, line):
    bias = refs.units[line : line + 1]
    rows_all = refs.hidden.held.shape[0]
    for rows in chunks(rows_all):
        hidden, slope = gelu_pair(nn(refs.low[rows], refs.w_up[...]) + bias)
        refs.hidden[rows] = hidden.astype(bf16)
        refs.slope[rows] = slope.astype(bf16)
        if rows.stop * 2 % rows_all == 0:
            refs.hidden.flush(rows.stop * 2 // rows_all - 1)
            refs.slope.flush(rows.stop * 2 // rows_all - 1)


def hidden_results(rows, units):
    made = ([(0, rows // 2), (rows // 2, rows)], (rows, units), bf16)
    return dict(hidden=made, slope=made)


def ffn_first(meta, line, norm, w_up, layer, units):
    rows, model = norm.base.shape

    def body(refs):
        norm_into(refs, norm.line)
        ffn_into(refs, line)

    operands = dict(meta=(SCALAR, meta)) | parts_in(norm)
    operands |= dict(
        base=(FAR, norm.base), vecs=(FAR, norm.vecs), w_up=(FAR, w_up, layer), units=(FAR, units)
    )
    return run("ffn", body, operands, norm_results(rows, model) | hidden_results(rows, w_up.shape[2]))


def ffn_second(meta, line, y_low, w_up, units, hidden_own, w_down_own, layer, w_down_par):
    rows, model = y_low.shape

    def body(refs):
        ffn_into(refs, line)
        for at, part in enumerate(chunks(rows)):
            made = nn(refs.hidden_own[part], refs.wd_own[...]) + nn(refs.hidden[part], refs.wd_par[...])
            getattr(refs, f"mine{at}")[...] = made.astype(bf16)

    operands = dict(
        meta=(SCALAR, meta),
        low=(FAR, y_low),
        w_up=w_up,
        units=(FAR, units),
        hidden_own=(FAR, hidden_own),
        wd_own=(FAR, w_down_own, layer),
        wd_par=w_down_par,
    )
    results = hidden_results(rows, w_up[1].shape[-1]) | parts_out(rows, model)
    return run("ffn", body, operands, results)


def norm_back_results(rows, width):
    return dict(
        g=(FAR, (rows, width), f32), low=(FAR, (rows, width), bf16), sums=(FAR, (8, width), f32)
    )


def ffn_back(meta, norm, kept, y_low, w_up, w_down, extra, other):
    rows, model = y_low.shape
    units = w_up[1].shape[-1]
    count = units + model + (0 if extra is None else extra.shape[0])
    first = norm is not None
    operands = dict(meta=(SCALAR, meta))
    operands |= norm.operands if first else dict(low=(FAR, other.low))
    operands |= dict(w_down=w_down, slope=(FAR, kept.slope), hidden=(FAR, kept.hidden), y=(FAR, y_low))
    if extra is not None:
        operands |= dict(extra=(FAR, extra))
    results = dict(
        grads=([(0, units), (units, count)], (count, model), bf16), line=(FAR, (8, units), f32)
    )
    if first:
        results |= norm_back_results(rows, model) | dict(pre=(FAR, (rows, units), bf16))
    else:
        operands |= dict(w_up=w_up, pre_other=(FAR, other.pre), w_up_other=other.w_up)
        results |= parts_out(rows, model)

    def body(refs):
        if first:
            norm_back_into(refs, norm.line)
            pre_ref = refs.pre
        else:
            pre_ref = refs.scratch[0]

        @stage
        def _():
            total = None
            for at in chunks(rows):
                pre = (refs.slope[at].astype(f32) * nt(refs.low[at], refs.w_down[...])).astype(bf16)
                pre_ref[at] = pre
                line = jnp.sum(pre.astype(f32), 0, keepdims=True)
                total = line if total is None else total + line
            if first:
                pre_ref.flush()
            refs.line[0:1] = total
            refs.line[1:] = jnp.zeros((7, units), f32)
            refs.line.flush()

        @stage
        def _():
            refs.grads[:units] = tn(refs.hidden[...], refs.low[...]).astype(bf16)
            refs.grads.flush(0)

        @stage
        def _():
            refs.grads[units : units + model] = tn(refs.y[...], pre_ref[...]).astype(bf16)
            if extra is not None:
                refs.grads[units + model :] = refs.extra[...]
            refs.grads.flush(1)

        if not first:

            @stage
            def _():
                for at, part in enumerate(chunks(rows)):
                    made = nt(pre_ref[part], refs.w_up[...]) + nt(refs.pre_other[part], refs.w_up_other[...])
                    getattr(refs, f"mine{at}")[...] = made.astype(bf16)

    scratch = () if first else (pltpu.VMEM((rows, units), bf16),)
    return run("ffn_back", body, operands, results, scratch=scratch)


def attend_back(meta, per, small, norm, kept, x_all, w_qkv, w_out, other, last):
    rows, model = x_all.shape
    width = w_out[1].shape[-2]
    half = rows // 2 - small
    first = norm is not None
    scale = HEAD**-0.5
    operands = dict(meta=(SCALAR, meta))
    operands |= norm.operands if first else dict(low=(FAR, other.low))
    operands |= dict(
        w_out=w_out,
        a=(FAR, kept.a),
        k=(FAR, kept.k),
        q=(FAR, kept.q),
        lse=(FAR, kept.lse),
        v=(FAR, kept.v),
        x=(FAR, x_all),
    )
    results = dict(
        grads=([(0, 3 * width), (3 * width, 4 * width)], (4 * width, model), bf16),
        line=(FAR, (8, 3 * width), f32),
    )
    if first:
        results |= norm_back_results(rows, model) | dict(g_qkv=(FAR, (rows, 3 * width), bf16))
    else:
        operands |= dict(w_qkv=w_qkv, g_other=(FAR, other.g_qkv), w_other=(FAR, other.w_qkv))
        if last:
            operands |= dict(g_norm=(FAR, other.g))
            results |= dict(own=(NEAR, (rows // 2, model), f32), away=(NEAR, (rows // 2, model), bf16))
        else:
            results |= parts_out(rows, model)
    scratch = [
        pltpu.VMEM((rows, width), bf16),
        pltpu.VMEM((2 * half, HEAD), f32),
        pltpu.VMEM((2 * half, HEAD), f32),
    ]
    if not first:
        scratch.append(pltpu.VMEM((rows, 3 * width), bf16))

    def body(refs):
        if first:
            norm_back_into(refs, norm.line)
            g_ref = refs.g_qkv
        else:
            g_ref = refs.scratch[3]
        da_ref, dv_sum, dk_sum = refs.scratch[:3]

        low = refs.low[...]
        da_ref[...] = nt(low, refs.w_out[...]).astype(bf16)
        refs.grads[3 * width :] = tn(refs.a[...], low).astype(bf16)
        refs.grads.flush(1)

        same = small_same(refs.meta, per, small)

        ones = jnp.ones((8, HEAD), f32)
        for head in range(width // HEAD):
            cols = slice(head * HEAD, (head + 1) * HEAD)
            line = slice(head, head + 1)
            k_head = refs.k[:, cols]
            v_head = refs.v[:, cols]
            q_head = refs.q[:, cols] * scale
            da_head = da_ref[:, cols]
            inner = da_head.astype(f32) * refs.a[:, cols].astype(f32)
            delta = exact(ones, inner, ((1,), (1,)))[0:1]
            k_long = long_rows(k_head, half, small)
            v_long = long_rows(v_head, half, small)
            k_long_t = (k_long * scale).T
            for count, at in enumerate(q_starts(half, small, Q_ROWS)):
                here = slice(at, at + Q_ROWS)
                q_blk = q_head[here]
                da_blk = da_head[here]
                probs = jnp.exp(nt(k_long, q_blk) - refs.lse[line, here])
                g_probs = nt(v_long, da_blk)
                g_scores = (probs * (g_probs - delta[:, here])).astype(bf16)
                g_v = nn(probs.astype(bf16), da_blk)
                g_k = nn(g_scores, q_blk)
                if count == 0:
                    dv_sum[...] = g_v
                    dk_sum[...] = g_k
                else:
                    dv_sum[...] += g_v
                    dk_sum[...] += g_k
                g_ref[here, cols] = nn(k_long_t, g_scores).T.astype(bf16)
            k_cols = slice(width + head * HEAD, width + (head + 1) * HEAD)
            v_cols = slice(2 * width + head * HEAD, 2 * width + (head + 1) * HEAD)
            for part, base in enumerate((0, half + small)):
                g_ref[base : base + half, k_cols] = dk_sum[part * half : (part + 1) * half].astype(bf16)
                g_ref[base : base + half, v_cols] = dv_sum[part * half : (part + 1) * half].astype(bf16)
            k_small = small_rows(k_head, half, small)
            q_small = small_rows(q_head, half, small)
            da_small = small_rows(da_head, half, small)
            lse = jnp.concatenate(
                [refs.lse[line, half : half + small], refs.lse[line, 2 * half + small :]], 1
            )
            delta = jnp.concatenate([delta[:, half : half + small], delta[:, 2 * half + small :]], 1)
            probs = jnp.exp(jnp.where(same, nt(k_small, q_small), MASKED) - lse)
            g_probs = nt(small_rows(v_head, half, small), da_small)
            g_scores = (probs * (g_probs - delta)).astype(bf16)
            for where, made in (
                (cols, nn((k_small * scale).T, g_scores).T),
                (k_cols, nn(g_scores, q_small)),
                (v_cols, nn(probs.astype(bf16), da_small)),
            ):
                g_ref[half : half + small, where] = made[:small].astype(bf16)
                g_ref[2 * half + small :, where] = made[small:].astype(bf16)

        if first:
            g_ref.flush()
        g_all = g_ref[...]
        refs.grads[: 3 * width] = tn(g_all, refs.x[...]).astype(bf16)
        refs.grads.flush(0)
        refs.line[0:1] = jnp.sum(g_all.astype(f32), 0, keepdims=True)
        refs.line[1:] = jnp.zeros((7, 3 * width), f32)
        refs.line.flush()

        if not first:
            core = facts(refs.meta, per)[0]
            place = row_places(refs.meta, per, half, small, 1)

            made = nn(g_ref[...], refs.w_qkv[...]) + nn(refs.g_other[...], refs.w_other[...])
            if last:
                own = rows // 2
                made = made + jnp.concatenate([refs.g_norm[:own], jnp.zeros((own, model), f32)], 0)
                high = made.astype(bf16)
                rest = (made - high.astype(f32)).astype(bf16)
                at = lax.broadcasted_iota(i32, (own, rows), 0)
                pick = (place == core * own + at).astype(bf16)
                refs.own[...] = nn(pick, high) + nn(pick, rest)
                refs.away[...] = nn((place == (1 - core) * own + at).astype(bf16), high).astype(bf16)
            else:
                for at, part in enumerate(chunks(rows)):
                    getattr(refs, f"mine{at}")[...] = made[part].astype(bf16)

    return run("attend_back", body, operands, results, scratch=scratch)


def halve(place, value, other):
    rows, width = value.shape[0] // 2, value.shape[1]
    kind = value.dtype
    if rows % 16:

        def take(which):
            return sum(
                lax.dynamic_slice_in_dim(part, which * rows, rows, 0).astype(f32) for part in (value, other)
            ).astype(kind)

        return take(place[0]), take(1 - place[0])

    def body(refs):
        place = refs.place[0]
        for out, which in ((refs.sent, 1 - place), (refs.kept, place)):
            part = pl.ds(pl.multiple_of(which * rows, 16), rows)
            out[...] = (refs.value[part].astype(f32) + refs.other[part].astype(f32)).astype(kind)

    made = (NEAR, (rows, width), kind)
    got = run(
        "halve",
        body,
        dict(place=(SCALAR, place), value=(NEAR, value), other=(NEAR, other)),
        dict(kept=made, sent=made),
    )
    return got.kept, got.sent


def join(place, mine, other):
    rows, width = mine.shape
    if rows % 16:
        return jnp.where(place[0] == 1, jnp.concatenate([other, mine], 0), jnp.concatenate([mine, other], 0))

    def body(refs):
        place = refs.place[0]
        refs.out[pl.ds(pl.multiple_of(place * rows, 16), rows)] = refs.mine[...]
        refs.out[pl.ds(pl.multiple_of((1 - place) * rows, 16), rows)] = refs.other[...]

    return run(
        "join",
        body,
        dict(place=(SCALAR, place), mine=(NEAR, mine), other=(NEAR, other)),
        dict(out=(NEAR, (2 * rows, width), mine.dtype)),
    ).out


def slices(meta, weights, strips, strip_rows):
    given = [*weights, *strips]
    model = given[-1][0].shape[2]

    def body(meta_ref, *refs):
        sems, outs = refs[-1], refs[len(given) : -1]
        copies = []
        for at, (_, layer) in enumerate(given):
            if at < len(weights):
                copies.append((refs[at].at[layer], outs[at]))
            else:
                rows = pl.ds(pl.multiple_of(meta_ref[0] * strip_rows, 16), strip_rows)
                part = pl.ds((at - len(weights)) * strip_rows, strip_rows)
                copies.append((refs[at].at[layer, rows], outs[-1].at[part]))
        copies = [pltpu.make_async_copy(*pair, sems.at[at]) for at, pair in enumerate(copies)]
        for copy in copies:
            copy.start()
        for copy in copies:
            copy.wait()

    made = [pltpu.VMEM(array.shape[1:], array.dtype) for array, _ in weights]
    made += [pltpu.VMEM((len(strips) * strip_rows, model), bf16)] if strips else []
    return pl.pallas_call(
        body,
        out_shape=tuple(made),
        in_specs=[SMEM] + [HBM] * len(given),
        out_specs=(VMEM,) * len(made),
        scratch_shapes=[pltpu.SemaphoreType.DMA((len(given),))],
        cost_estimate=pl.CostEstimate(flops=COST, transcendentals=0, bytes_accessed=0),
        name="slices",
    )(meta, *[pltpu.with_memory_space_constraint(array, pltpu.HBM) for array, _ in given])


def gather_small(meta, per, b_out, b_down, ln_gain, ln_shift, b_up, b_qv, queries):
    layers, units = b_up.shape
    model = b_out.shape[1]
    width = b_qv.shape[2]
    q_group, q_piece, dim = queries.shape
    q_rows = q_group * q_piece

    def body(meta, bo_ref, bd_ref, gain_ref, shift_ref, bu_ref, bqv_ref, q_ref, vec_out, line_out, carried_out):
        vec_out[...] = jnp.zeros(vec_out.shape, f32)
        line_out[...] = jnp.zeros(line_out.shape, f32)
        for layer in range(layers):
            for at, ref in ((0, bo_ref), (1, bd_ref)):
                first = 8 * (2 * layer + at)
                vec_out[first : first + 1] = ref[layer : layer + 1]
                vec_out[first + 1 : first + 2] = gain_ref[layer, at : at + 1]
                vec_out[first + 2 : first + 3] = shift_ref[layer, at : at + 1]
                line_out[2 * layer + 1 : 2 * layer + 2, at * width : (at + 1) * width] = bqv_ref[
                    layer, at : at + 1
                ]
            line_out[2 * layer : 2 * layer + 1] = bu_ref[layer : layer + 1].astype(f32)
        for at in range(q_group):
            carried_out[at * q_piece : (at + 1) * q_piece] = q_ref[at]
        lane = lax.broadcasted_iota(i32, (CARRIED - q_rows, dim), 1)
        row = lax.broadcasted_iota(i32, (CARRIED - q_rows, dim), 0)
        made = jnp.zeros((CARRIED - q_rows, dim), f32)
        for at in range(2 * per):
            made = jnp.where((lane == at) & (row == 0), meta[2 + 2 * per + at].astype(f32), made)
        carried_out[q_rows:] = made.astype(bf16)

    return pl.pallas_call(
        body,
        out_shape=(
            jax.ShapeDtypeStruct((16 * layers, model), f32),
            jax.ShapeDtypeStruct((-(-2 * layers // 8) * 8, units), f32),
            jax.ShapeDtypeStruct((CARRIED, dim), bf16),
        ),
        in_specs=[SMEM] + [VMEM] * 7,
        out_specs=(VMEM,) * 3,
        cost_estimate=pl.CostEstimate(flops=COST, transcendentals=0, bytes_accessed=0),
        name="gather_small",
    )(meta, b_out, b_down, ln_gain, ln_shift, b_up, b_qv, queries)


def turn(meta, per, small, x_own, x_other):
    own, model = x_own.shape
    rows = 2 * own

    def body(refs):
        core = facts(refs.meta, per)[0]
        place = row_places(refs.meta, per, own - small, small, 0)
        at = lax.broadcasted_iota(i32, (rows, own), 1)
        made = nn((place == core * own + at).astype(bf16), refs.mine[...])
        made = made + nn((place == (1 - core) * own + at).astype(bf16), refs.came[...])
        made = made.astype(bf16)
        refs.near[...] = made
        refs.low[...] = made
        refs.low.flush()

    operands = dict(meta=(SCALAR, meta), mine=(NEAR, x_own), came=(NEAR, x_other))
    results = dict(near=(NEAR, (rows, model), bf16), low=(FAR, (rows, model), bf16))
    return run("turn", body, operands, results)


CARRIED = 32


def query_of(at, q_group, q_piece):
    return at // q_piece % q_group


def score(meta, per, small, norm, w_proj, carried, q_group, q_piece, n_mp):
    rows, model = norm.base.shape
    half = rows // 2 - small
    dim = w_proj.shape[1]
    q_rows = q_group * q_piece
    q_tok = q_rows * n_mp
    count = per * q_tok
    n_dp = carried.shape[0] // (n_mp * CARRIED)

    def body(refs):
        norm_into(refs, norm.line)
        groups = facts(refs.meta, per)[4]
        for at in range(per):
            for piece in range(n_mp):
                side = piece % 2 * 2 + piece // 2
                source = pl.multiple_of((side * n_dp + groups[at]) * CARRIED, CARRIED)
                first = at * q_tok + piece * q_rows
                refs.flat_q[first : first + q_rows] = refs.carried[pl.ds(source, q_rows)]
        emb = nn(refs.low[...], refs.w_proj[...])
        unit = emb * lax.rsqrt(jnp.sum(emb * emb, -1, keepdims=True) + UNIT_EPS)
        segment = row_segments(refs.meta, per, half, small)
        owner = lax.broadcasted_iota(i32, (rows, count), 1) // q_tok == segment
        similar = nt(unit.astype(bf16), refs.flat_q[...])
        terms = jnp.where(owner, jnp.exp(SHARP * (similar - 1.0)), 0.0)
        totals = jnp.sum(terms, 0, keepdims=True)
        refs.totals[...] = jnp.broadcast_to(totals, (8, count))
        _, micro, _, _, _ = facts(refs.meta, per)
        slot = (refs.meta[0] * 2 + micro) * per
        lane = lax.broadcasted_iota(i32, (8, count), 1)
        length = jnp.zeros((8, count), f32)
        for at in range(per):
            size = jnp.full((8, count), refs.meta[2 + micro * per + at].astype(f32))
            length = jnp.where(lane // q_tok == at, size, length)
        term = (jnp.log(jnp.broadcast_to(totals, (8, count))) - jnp.log(length)) / SHARP + 1.0
        row = lax.broadcasted_iota(i32, (8, count), 0)
        term = jnp.where(query_of(lane, q_group, q_piece) == row, term, 0.0)
        n_pass = refs.logits.shape[1]
        target = lax.broadcasted_iota(i32, (count, n_pass), 1)
        source = lax.broadcasted_iota(i32, (count, n_pass), 0)
        pick = (source // q_tok + slot == target).astype(f32)
        refs.logits[...] = exact(term, pick) / TEMPER

    n_pass = carried.shape[0] // (n_mp * CARRIED) * 2 * per
    operands = dict(meta=(SCALAR, meta)) | parts_in(norm)
    operands |= dict(
        base=(FAR, norm.base),
        vecs=(FAR, norm.vecs),
        carried=(NEAR, carried),
        w_proj=(FAR, w_proj),
    )
    results = norm_results(rows, model, keep=False) | dict(
        flat_q=(NEAR, (count, dim), bf16),
        totals=(NEAR, (8, count), f32),
        logits=(NEAR, (8, n_pass), f32),
    )
    return run("score", body, operands, results)


def loss_back(meta, per, small, logits, groups, targets, totals, flat_q, final, w_proj, q_group, q_piece, n_mp):
    n_dp, n_pass = targets.shape[1], logits.shape[1]
    rows, model = final.shape
    half = rows // 2 - small
    dim = w_proj.shape[1]
    q_rows = q_group * q_piece
    q_tok = q_rows * n_mp
    count = per * q_tok
    held = n_dp * q_rows * (n_mp // 2)

    def body(refs):
        meta = refs.meta
        core, micro, _, _, own_groups = facts(meta, per)
        member = refs.groups[...] == lax.broadcasted_iota(i32, (n_dp, n_pass), 0)
        lane = lax.broadcasted_iota(i32, (n_dp, n_pass), 1)
        g_rows = []
        for query in range(q_group):
            logit = refs.logits[query : query + 1]
            spread = jnp.where(member, logit, FLOOR)
            top = jnp.max(spread, 1, keepdims=True)
            mass = jnp.sum(jnp.where(member, jnp.exp(spread - top), 0.0), 1, keepdims=True)
            lse = top + jnp.log(mass)
            hit = lane == refs.targets[query]
            refs.loss[query] = lse - jnp.sum(jnp.where(hit, logit, 0.0), 1, keepdims=True)
            lse_pass = jnp.sum(jnp.where(member, lse, 0.0), 0, keepdims=True)
            hits = jnp.sum(jnp.where(hit & member, 1.0, 0.0), 0, keepdims=True)
            g_rows.append(jnp.exp(logit - lse_pass) - hits)
        g_logit = jnp.concatenate(g_rows + [jnp.zeros((8 - q_group, n_pass), f32)], 0)
        slot = (meta[0] * 2 + micro) * per
        lane = lax.broadcasted_iota(i32, (n_pass, count), 0)
        at = lax.broadcasted_iota(i32, (n_pass, count), 1)
        wide = exact(g_logit, (at // q_tok + slot == lane).astype(f32))
        at = lax.broadcasted_iota(i32, (8, count), 1)
        row = lax.broadcasted_iota(i32, (8, count), 0)
        wide = jnp.where(query_of(at, q_group, q_piece) == row, wide, 0.0)
        wide = jnp.sum(wide, 0, keepdims=True)
        g_total = (wide / TEMPER) / (SHARP * refs.totals[0:1])
        low = refs.final[...]
        emb = nn(low, refs.w_proj[...])
        scale = lax.rsqrt(jnp.sum(emb * emb, -1, keepdims=True) + UNIT_EPS)
        unit = emb * scale
        unit_low = unit.astype(bf16)
        segment = row_segments(meta, per, half, small)
        owner = lax.broadcasted_iota(i32, (rows, count), 1) // q_tok == segment
        similar = nt(unit_low, refs.flat_q[...])
        terms = jnp.where(owner, jnp.exp(SHARP * (similar - 1.0)), 0.0)
        g_sim = (SHARP * terms * g_total).astype(bf16)
        g_unit = nn(g_sim, refs.flat_q[...])
        g_emb = scale * (g_unit - unit * jnp.sum(g_unit * unit, -1, keepdims=True))
        g_emb = g_emb.astype(bf16)
        refs.grad[...] = nt(g_emb, refs.w_proj[...])
        refs.proj[...] = tn(g_emb, low).astype(bf16)
        g_picked = tn(g_sim, unit_low)
        row = lax.broadcasted_iota(i32, (held, count), 0)
        source = lax.broadcasted_iota(i32, (held, count), 1)
        group = row // q_rows % n_dp
        piece = row // (q_rows * n_dp) * 2 + core
        want = piece * q_rows + row % q_rows
        line = lax.broadcasted_iota(i32, (1, count), 1) // q_tok
        source_group = jnp.zeros((1, count), i32)
        for passage in range(per):
            source_group = jnp.where(line == passage, own_groups[passage], source_group)
        pick = ((source % q_tok == want) & (source_group == group)).astype(f32)
        refs.queries[...] = exact(pick, g_picked)

    operands = dict(
        meta=(SCALAR, meta),
        logits=(NEAR, logits),
        groups=(NEAR, groups),
        targets=(NEAR, targets),
        totals=(NEAR, totals),
        flat_q=(NEAR, flat_q),
        final=(FAR, final),
        w_proj=(FAR, w_proj),
    )
    results = dict(
        loss=(NEAR, (q_group, n_dp, 1), f32),
        queries=(NEAR, (held, dim), f32),
        proj=(NEAR, (dim, model), bf16),
        grad=(NEAR, (rows, model), f32),
    )
    return run("loss_back", body, operands, results)


def pack(meta, sums, own, par):
    model = sums[0].shape[1]
    first = 8 * len(sums)
    rows = first + -(-2 * len(own) // 8) * 8
    operands = dict(meta=(SCALAR, meta)) | {f"sum{at}": (FAR, value) for at, value in enumerate(sums)}
    for layer, pairs in enumerate(zip(own, par)):
        for side, pair in enumerate(pairs):
            for at, value in enumerate(pair):
                operands[f"line{layer}{side}{at}"] = (FAR, value)

    def body(refs):
        for side, out in enumerate((refs.own, refs.par)):
            out[first:] = jnp.zeros((rows - first, model), f32)
            for at in range(len(sums)):
                out[8 * at : 8 * at + 8] = getattr(refs, f"sum{at}")[...]
            for layer in range(len(own)):
                for at in range(2):
                    value = getattr(refs, f"line{layer}{side}{at}")
                    row = first + 2 * layer + at
                    out[row : row + 1, : value.held.shape[1]] = value[0:1]

    made = (NEAR, (rows, model), f32)
    got = run("pack", body, operands, dict(own=made, par=made))
    return got.own, got.par


def quarters(place, value, other):
    rows, width = value.shape[0] // 4, value.shape[1]

    def body(refs):
        for at in (1, 2, 3, 0):
            part = pl.ds(pl.multiple_of((refs.place[0] ^ at) * rows, 16), rows)
            made = refs.value[part].astype(f32) + refs.other[part].astype(f32)
            getattr(refs, f"part{at}")[...] = made.astype(value.dtype)

    operands = dict(place=(SCALAR, place), value=(NEAR, value), other=(NEAR, other))
    results = {f"part{at}": (NEAR, (rows, width), value.dtype) for at in range(4)}
    got = run("quarters", body, operands, results)
    return [getattr(got, f"part{at}") for at in range(4)]


def join_quarters(place, *parts):
    rows, width = parts[0].shape

    def body(refs):
        for at in range(4):
            part = pl.ds(pl.multiple_of((refs.place[0] ^ at) * rows, 16), rows)
            refs.out[part] = getattr(refs, f"part{at}")[...]

    operands = dict(place=(SCALAR, place)) | {f"part{at}": (NEAR, part) for at, part in enumerate(parts)}
    return run("join", body, operands, dict(out=(NEAR, (4 * rows, width), parts[0].dtype))).out


def store(layer, layers, parts, before):
    count = len(parts)
    model = parts[0][0].shape[1]
    sources = []
    for array, _, _ in parts:
        if all(array is not other for other in sources):
            sources.append(array)

    def body(*refs):
        outs = refs[len(sources) + (count if before else 0) :][:count]
        held, sems = refs[-1 - count : -1], refs[-1]
        for at, (array, first, rows) in enumerate(parts):
            source = [ref for ref, given in zip(refs, sources) if given is array][0]
            held[at][...] = source[first : first + rows].astype(f32)
            pltpu.make_async_copy(held[at], outs[at].at[layer], sems.at[at]).start()
        for at in range(count):
            pltpu.make_async_copy(held[at], outs[at].at[layer], sems.at[at]).wait()

    given = [pltpu.with_memory_space_constraint(value, pltpu.VMEM) for value in sources]
    if before:
        given += [pltpu.with_memory_space_constraint(value, pltpu.HBM) for value in before]
    return pl.pallas_call(
        body,
        out_shape=tuple(pltpu.HBM((layers, rows, model), f32) for _, _, rows in parts),
        in_specs=[VMEM] * len(sources) + [HBM] * (count if before else 0),
        out_specs=(HBM,) * count,
        scratch_shapes=[pltpu.VMEM((rows, model), f32) for _, _, rows in parts]
        + [pltpu.SemaphoreType.DMA((count,))],
        input_output_aliases={len(sources) + at: at for at in range(count)} if before else {},
        compiler_params=pltpu.CompilerParams(vmem_limit_bytes=VMEM_LIMIT),
        cost_estimate=pl.CostEstimate(flops=COST, transcendentals=0, bytes_accessed=0),
        name="store",
    )(*given)


def add(*parts):
    def body(refs):
        total = sum(getattr(refs, f"part{at}")[...].astype(f32) for at in range(len(parts)))
        refs.out[...] = total.astype(parts[0].dtype)

    operands = {f"part{at}": (NEAR, part) for at, part in enumerate(parts)}
    return run("add", body, operands, dict(out=(NEAR, parts[0].shape, parts[0].dtype))).out


def on_device(
    passages_in,
    queries,
    w_qkv,
    b_qv,
    w_out,
    b_out,
    ln_gain,
    ln_shift,
    w_up,
    b_up,
    w_down,
    b_down,
    w_proj,
    lengths,
    passage_group,
    positive,
):
    n_mp = lax.axis_size("mp")
    n_dp = lax.axis_size("dp")
    own, model = passages_in.shape
    micro_count, per = lengths.shape
    tok_mb = own * n_mp // micro_count
    assert n_mp == 4 and micro_count == 2 and n_dp & (n_dp - 1) == 0
    layers = w_qkv.shape[0]
    width = w_qkv.shape[3]
    ff = w_up.shape[2]
    small = (tok_mb - LONGEST) // 2
    q_group, q_piece, dim = queries.shape
    q_rows = q_group * q_piece

    mp_here = lax.axis_index("mp")
    dp_here = lax.axis_index("dp")
    core, micro = mp_here % 2, mp_here // 2
    dp_bits = [1 << at for at in range(n_dp.bit_length() - 1)]

    def to_pair(value):
        return jax.tree.map(lambda part: lax.ppermute(part, "mp", [(at, at ^ 1) for at in range(n_mp)]), value)

    def to_x(value):
        return lax.ppermute(value, "mp", [(at, at ^ 2) for at in range(n_mp)])

    def to_dp(value, bit):
        return lax.ppermute(value, "dp", [(at, at ^ bit) for at in range(n_dp)])

    noted = []

    def here(value):
        return lax.optimization_barrier((value, noted[-1]))[0] if noted else value

    def note(value):
        noted.append(value)
        return value

    meta = jnp.concatenate(
        [jnp.stack([dp_here, mp_here]).astype(i32), lengths.reshape(-1), passage_group.reshape(-1)]
    )
    core_place, micro_place = core[None].astype(i32), micro[None].astype(i32)
    places = {bit: ((dp_here // bit) % 2)[None].astype(i32) for bit in dp_bits}

    w_qkv = w_qkv.transpose(0, 2, 3, 1).reshape(layers, 3 * width, model)
    x_other = to_pair(passages_in)
    strip_rows = model // n_dp

    def strips_of(meta, pairs):
        if strip_rows % 16 == 0:
            return slices(meta, [], pairs, strip_rows)[0]
        parts = [
            lax.dynamic_slice_in_dim(array[layer], dp_here * strip_rows, strip_rows, 0) for array, layer in pairs
        ]
        return jnp.concatenate(parts, 0)

    def gathered(strip):
        count = strip.shape[0] // strip_rows
        stack = lax.all_gather(strip, "dp", axis=0)
        if strip_rows % 16:
            parts = [stack[:, at * strip_rows : (at + 1) * strip_rows] for at in range(count)]
            return [(FAR, part.reshape(-1, model)) for part in parts]
        return [
            (FAR, stack, (slice(None), slice(at * strip_rows, (at + 1) * strip_rows))) for at in range(count)
        ]

    def after(value, first):
        return lax.optimization_barrier((value, first))[0]

    strip = strips_of(meta, [(w_up, 0), (w_down, 0)])
    strip_par = to_x(strip)
    turned = turn(after(meta, strip), per, small, passages_in, x_other)
    vecs, lines, first_carried = gather_small(
        after(meta, turned.low), per, b_out, b_down, ln_gain, ln_shift, b_up, b_qv, queries
    )
    lines_par = to_x(lines)
    sent = slices(after(meta, lines), [(w_qkv, 0), (w_out, 0)], [], strip_rows)
    w_par = [SimpleNamespace() for _ in range(layers)]
    w_par[0].up, w_par[0].down = gathered(after(strip_par, sent[0]))
    w_par[0].qkv, w_par[0].out = (to_x(after(value, lines_par)) for value in sent)

    def spread():
        value = first_carried
        steps = [((lambda v, bit=bit: to_dp(v, bit)), places[bit]) for bit in dp_bits]
        steps += [(to_x, micro_place), (to_pair, core_place)]
        for send, place in steps:
            other = send(value)
            yield
            value = note(join(here(place), value, other))
        yield value

    spreading, spread_out = spread(), []

    def spread_on():
        spread_out.append(next(spreading, None))

    spread_on()

    x_all, base, norm = turned.low, turned.low, None
    stored = []
    for layer in range(layers):
        par = w_par[layer]
        att_own = attend_first(
            here(meta), per, small, 2 * layer + 1, turned.near if norm is None else None, norm, w_qkv, layer, lines
        )
        note(att_own.lse)
        if layer == 0:
            spread_on()
        if norm is not None:
            x_all, base = att_own.low, att_own.y
        att_par = attend_second(
            here(meta), per, small, 2 * layer + 1, x_all, par.qkv, lines_par, att_own.a, w_out, layer, par.out
        )
        note(att_par.lse)
        if layer + 1 < layers:
            strip_par = to_x(strips_of(here(meta), [(w_up, layer + 1), (w_down, layer + 1)]))
        norm = SimpleNamespace(
            mine=parts_of(att_par), came=to_pair(parts_of(att_par)), base=base, vecs=vecs, line=2 * layer
        )
        spread_on()
        ffn_own = ffn_first(here(meta), 2 * layer, norm, w_up, layer, lines)
        note(ffn_own.r)
        if layer != 0:
            spread_on()
        if layer + 1 < layers:
            at = layer + 1
            w_par[at].up, w_par[at].down = gathered(here(strip_par))
            pieces = slices(here(meta), [(w_qkv, at), (w_out, at)], [], strip_rows)
            w_par[at].qkv, w_par[at].out = (to_x(value) for value in pieces)
        ffn_par = ffn_second(
            here(meta), 2 * layer, ffn_own.low, par.up, lines_par, ffn_own.hidden, w_down, layer, par.down
        )
        note(ffn_par.mine0)
        norm = SimpleNamespace(
            mine=parts_of(ffn_par),
            came=to_pair(parts_of(ffn_par)),
            base=ffn_own.y,
            vecs=vecs,
            line=2 * layer + 1,
        )
        if layer == 0:
            spread_on()
        stored.append([x_all, att_own, att_par, ffn_own, ffn_par])
    spread_out += list(spreading)
    carried = next(value for value in spread_out if value is not None)
    groups = carried.reshape(n_mp, n_dp, CARRIED, dim)[0, :, q_rows, : passage_group.size]
    groups = groups.reshape(1, -1).astype(i32)

    found = score(here(meta), per, small, norm, w_proj, carried, q_group, q_piece, n_mp)
    norms_after = [stored[layer][1] for layer in range(1, layers)] + [found]
    logits = found.logits
    logits = logits + to_x(logits)
    for bit in dp_bits:
        logits = logits + to_dp(logits, bit)
    back = loss_back(
        meta,
        per,
        small,
        logits,
        groups,
        positive.reshape(n_dp, q_group).T[:, :, None],
        found.totals,
        found.flat_q,
        found.low,
        w_proj,
        q_group,
        q_piece,
        n_mp,
    )
    note(back.grad)
    query_loss = lax.dynamic_index_in_dim(back.loss[:, :, 0], dp_here, 1, keepdims=False)

    def total(theirs):
        other = to_x(here(theirs))
        value = yield
        yield
        for bit in dp_bits:
            value, sent = halve(here(places[bit]), value, other)
            note(value)
            other = to_dp(sent, bit)
            yield
        value = note(add(here(value), other))
        for bit in reversed(dp_bits):
            other = to_dp(value, bit)
            yield
            value = note(join(here(places[bit]), value, other))
        yield value

    def total_early(theirs):
        other = to_x(here(theirs))
        value = yield
        yield
        value, sent = halve(here(places[1]), value, other)
        note(value)
        other = to_dp(sent, 1)
        yield
        value = note(add(here(value), other))
        value = lax.psum(value, "dp", axis_index_groups=[list(range(side, n_dp, 2)) for side in range(2)])
        yield
        value = note(here(value))
        yield
        value = here(value)
        other = to_dp(value, 1)
        yield
        yield note(join(here(places[1]), value, other))

    def query_sums():
        value = back.queries
        rows = value.shape[0] // 2
        other = to_x(lax.dynamic_slice_in_dim(value, (1 - micro) * rows, rows, 0))
        value = lax.dynamic_slice_in_dim(value, micro * rows, rows, 0)
        for bit in reversed(dp_bits):
            yield
            value, sent = halve(here(places[bit]), value, other)
            note(value)
            other = to_dp(sent, bit)
        yield
        yield note(add(here(value), other))

    queried = query_sums()
    next(queried)
    running = []

    def advance(which, count=1):
        for _ in range(count):
            got = next(running[which])
        return got

    finals = [None] * (2 * layers)
    rep_sums, own_sums, par_sums = [None] * (2 * layers), [None] * layers, [None] * layers
    grads = dict(grad=(NEAR, back.grad))
    for layer in reversed(range(layers)):
        x_all, att_own, att_par, ffn_own, ffn_par = stored[layer]
        par = w_par[layer]
        last = layer == layers - 1
        extra = back.proj if last else None

        def way(line, kept):
            rest = dict(n=(FAR, kept.n), r=(FAR, kept.r), vecs=(FAR, vecs))
            return SimpleNamespace(operands=grads | rest, line=line)

        got_par = ffn_back(
            here(meta),
            way(2 * layer + 1, norms_after[layer]),
            ffn_par,
            ffn_own.low,
            par.up,
            par.down,
            extra,
            None,
        )
        note(got_par.line)
        if last:
            next(queried)
        else:
            advance(0)
            advance(1)
        running.append((total_early if last else total)(got_par.grads))
        advance(-1)
        other = SimpleNamespace(low=got_par.low, pre=got_par.pre, w_up=par.up)
        got_own = ffn_back(
            here(meta), None, ffn_own, ffn_own.low, (FAR, w_up, layer), (FAR, w_down, layer), extra, other
        )
        note(got_own.line)
        running[-1].send(got_own.grads)
        rep_sums[2 * layer + 1] = got_par.sums
        bup = (got_own.line, got_par.line)
        exchanged = SimpleNamespace(mine=parts_of(got_own), came=to_pair(parts_of(got_own)))
        grads = parts_in(exchanged) | dict(base=(FAR, got_par.g))
        if last:
            next(queried)
        else:
            advance(1)
        got_par = attend_back(
            here(meta),
            per,
            small,
            way(2 * layer, ffn_own),
            att_par,
            x_all,
            (FAR, par.qkv),
            (FAR, par.out),
            None,
            False,
        )
        note(got_par.line)
        if not last:
            advance(2)
            advance(1)
            advance(0)
        running.append(total(got_par.grads))
        advance(-1)
        if last:
            next(queried)
        other = SimpleNamespace(low=got_par.low, g_qkv=got_par.g_qkv, w_qkv=par.qkv, g=got_par.g)
        got_own = attend_back(
            here(meta), per, small, None, att_own, x_all, (FAR, w_qkv, layer), (FAR, w_out, layer), other, layer == 0
        )
        note(got_own.line)
        running[-1].send(got_own.grads)
        rep_sums[2 * layer] = got_par.sums
        own_sums[layer] = (bup[0], got_own.line)
        par_sums[layer] = (bup[1], got_par.line)
        if layer:
            exchanged = SimpleNamespace(mine=parts_of(got_own), came=to_pair(parts_of(got_own)))
            grads = parts_in(exchanged) | dict(base=(FAR, got_par.g))
        if last:
            query_grad = [value for value in queried if value is not None][0].reshape(q_group, q_piece, dim)
            advance(0)
    input_grad = got_own.own + to_pair(got_own.away).astype(f32)

    count = 2 * layers * 8
    flat, flat_par = pack(here(meta), rep_sums, own_sums, par_sums)
    flat_other = to_x(flat_par)

    def flat_sums():
        value, other = flat, flat_other
        for bit in dp_bits:
            yield
            value = note(add(here(value), other))
            other = to_dp(value, bit)
        yield
        yield note(add(here(value), other))

    running.append(flat_sums())
    advance(-1)
    finals = [None] * len(running)
    turns = TURNS if n_dp == 8 and layers == 2 else []
    for which in turns:
        finals[which] = advance(which)
    for which in range(len(running)):
        for got in running[which]:
            finals[which] = got
    flat = finals.pop()
    made = None
    for layer in reversed(range(layers)):
        ffn_sums, att_sums = finals[2 * (layers - 1 - layer) : 2 * (layers - layer)]
        if layer == layers - 1:
            g_wproj = ffn_sums[ff + model :].astype(f32).T
        parts = [(att_sums, 0, 3 * width), (att_sums, 3 * width, width), (ffn_sums, ff, model), (ffn_sums, 0, ff)]
        made = store(layer, layers, parts, made)
    g_wqkv, g_wout, g_wup, g_wdown = made
    norms = flat[:count].reshape(layers, 2, 8, model)
    units = flat[count : count + 2 * layers].reshape(layers, 2, model)
    g_bqv = jnp.stack([units[:, 1, :width], units[:, 1, 2 * width : 3 * width]], 1)
    g_wqkv = g_wqkv.reshape(layers, 3, width, model).transpose(0, 3, 1, 2)
    return (
        query_loss,
        input_grad,
        query_grad,
        g_wqkv,
        g_bqv,
        g_wout,
        norms[:, 0, 2],
        norms[:, :, 0],
        norms[:, :, 1],
        g_wup,
        units[:, 0],
        g_wdown,
        norms[:, 1, 2],
        g_wproj,
    )


def solution(mesh):
    placed = (
        P(("dp", "mp"), None),
        P("dp", "mp", None),
        P(None, None, None, "mp"),
        P(None, None, "mp"),
        P(None, "mp", None),
        P(),
        P(),
        P(),
        P(None, None, "mp"),
        P(None, "mp"),
        P(None, "mp", None),
        P(),
        P(),
        P("dp", None),
        P("dp", None),
        P(),
    )
    return jax.shard_map(
        on_device,
        mesh=mesh,
        in_specs=placed,
        out_specs=(
            P("dp"),
            P(("dp", "mp"), None),
            P("dp", "mp", None),
            P(None, None, None, "mp"),
            P(None, None, "mp"),
            P(None, "mp", None),
            P(),
            P(),
            P(),
            P(None, None, "mp"),
            P(None, "mp"),
            P(None, "mp", None),
            P(),
            P(),
        ),
        check_vma=False,
    )
```

```python
from types import SimpleNamespace

import jax
import jax.numpy as jnp
from jax import lax
from jax.experimental import pallas as pl
from jax.experimental.pallas import tpu as pltpu
from jax.sharding import PartitionSpec as P

HEAD = 64
LONGEST = 1024
SHARP = 4.0
TEMPER = 0.2
LN_EPS = 1e-12
UNIT_EPS = 1e-06
MASKED = -1000000000.0
FLOOR = -1e30
Q_ROWS = 512
AHEAD = 3
COST = 5000000
TURNS = (2, 3, 1, 4, 2, 3, 0, 1, 2, 3, 1, 2, 3, 2, 0, 1, 4, 3, 4, 3, 4, 2, 3)
VMEM_LIMIT = 40 * 2**20

bf16 = jnp.bfloat16
f32 = jnp.float32
i32 = jnp.int32
HIGH = lax.Precision.HIGHEST
VMEM = pl.BlockSpec(memory_space=pltpu.VMEM)
SMEM = pl.BlockSpec(memory_space=pltpu.SMEM)
HBM = pl.BlockSpec(memory_space=pltpu.HBM)
NEAR, FAR, SCALAR = range(3)


def nn(left_side, right_side):
    return lax.dot_general(
        left_side, right_side, (((1,), (0,)), ((), ())), preferred_element_type=f32
    )


def nt(left_side, right_side):
    return lax.dot_general(
        left_side, right_side, (((1,), (1,)), ((), ())), preferred_element_type=f32
    )


def tn(left_side, right_side):
    return lax.dot_general(
        left_side, right_side, (((0,), (0,)), ((), ())), preferred_element_type=f32
    )


def exact(left_side, right_side, dims=((1,), (0,))):
    return lax.dot_general(
        left_side, right_side, (dims, ((), ())), precision=HIGH, preferred_element_type=f32
    )


def gelu_pair(values):
    size = jnp.abs(values)
    t = 1.0 / (1.0 + (0.3275911 * 0.7071067811865476) * size)
    bell = jnp.exp(-0.5 * values * values)
    poly = t * (
        0.254829592
        + t * (-0.284496736 + t * (1.421413741 + t * (-1.453152027 + t * 1.061405429)))
    )
    tail = 0.5 * poly * bell
    phi = jnp.where(values < 0, tail, 1.0 - tail)
    return values * phi, phi + values * (0.3989422804014327 * bell)


class Fetched:
    def __init__(self, ref, part, held, sems, count, line):
        self.where = (ref, part, held, sems, count)
        self.held, self.line, self.due = held, line, True
        line.append(self)

    def copy(self):
        ref, part, held, sems, count = self.where
        return pltpu.make_async_copy(ref.at[part[0]] if part else ref, held, sems.at[count])

    def begin(self):
        self.line.remove(self)
        self.copy().start()

    def __getitem__(self, at):
        if self.due:
            if self in self.line:
                self.begin()
            if self.line:
                self.line[0].begin()
            self.copy().wait()
            self.due = False
        value = self.held[at]
        return value.reshape(-1, value.shape[-1]) if value.ndim == 3 else value


class Flushed:
    def __init__(self, ref, held, sems, pieces):
        self.ref, self.held, self.sems, self.pieces = ref, held, sems, pieces
        self.sent = []

    def __getitem__(self, at):
        return self.held[at]

    def __setitem__(self, at, value):
        self.held[at] = value

    def copy(self, which):
        first, last = self.pieces[which]
        rows = pl.ds(first, last - first)
        return pltpu.make_async_copy(self.held.at[rows], self.ref.at[rows], self.sems.at[which])

    def flush(self, which=0):
        self.copy(which).start()
        self.sent.append(which)


def stage(body):
    pl.when(lax.axis_index("dp") >= 0)(body)


def part_shape(shape, part=()):
    if isinstance(part, int):
        return shape[1:]
    return tuple(len(range(*at.indices(size))) for at, size in zip(part, shape)) + shape[len(part) :]


def run(name, body, operands, results, scratch=()):
    spaces = (pltpu.VMEM, pltpu.HBM)
    kinds = [given[0] for given in operands.values()]
    arrays = [
        given[1] if given[0] == SCALAR else pltpu.with_memory_space_constraint(given[1], spaces[given[0]])
        for given in operands.values()
    ]
    parts = [given[2:] for given in operands.values()]
    fetch = [at for at, kind in enumerate(kinds) if kind == FAR]
    made = list(results.values())
    pieces = {}
    for at, (kind, shape, _) in enumerate(made):
        if kind != NEAR:
            pieces[at] = [(0, shape[0])] if kind == FAR else kind
    added = [pltpu.VMEM(part_shape(arrays[at].shape, *parts[at]), arrays[at].dtype) for at in fetch]
    added += [pltpu.VMEM(made[at][1], made[at][2]) for at in pieces]
    added += [pltpu.SemaphoreType.DMA((max(len(fetch), 1),))]
    added += [pltpu.SemaphoreType.DMA((len(rows),)) for rows in pieces.values()]

    def outer(*refs):
        refs = list(refs)
        first = len(refs) - len(added)
        extra, refs = refs[first:], refs[:first]
        sems = extra[len(fetch) + len(pieces) :]
        line = []
        for count, at in enumerate(fetch):
            refs[at] = Fetched(refs[at], parts[at], extra[count], sems[0], count, line)
        for _ in range(min(AHEAD, len(line))):
            line[0].begin()
        outs = []
        for count, (at, rows) in enumerate(pieces.items()):
            out = Flushed(refs[len(operands) + at], extra[len(fetch) + count], sems[1 + count], rows)
            refs[len(operands) + at] = out
            outs.append(out)
        named = SimpleNamespace(scratch=refs[len(operands) + len(results) :])
        for key, ref in zip(list(operands) + list(results), refs):
            setattr(named, key, ref)
        body(named)
        for at in fetch:
            refs[at][0:1]
        for out in outs:
            for which in out.sent:
                out.copy(which).wait()

    given = pl.pallas_call(
        outer,
        out_shape=tuple(spaces[kind != NEAR](shape, dtype) for kind, shape, dtype in made),
        in_specs=[(VMEM, HBM, SMEM)[kind] for kind in kinds],
        out_specs=tuple(VMEM if kind == NEAR else HBM for kind, _, _ in made),
        scratch_shapes=list(scratch) + added,
        compiler_params=pltpu.CompilerParams(vmem_limit_bytes=VMEM_LIMIT),
        cost_estimate=pl.CostEstimate(flops=COST, transcendentals=0, bytes_accessed=0),
        name=name,
    )(*arrays)
    return SimpleNamespace(**dict(zip(results, given)))


def facts(meta, per):
    core, micro = meta[1] & 1, meta[1] >> 1
    ends, begin, last = [], 0, 0
    for at in range(per):
        length = meta[2 + micro * per + at]
        begin = begin + (length == LONGEST).astype(i32) * last
        last = last + length
        ends.append(last)
    groups = [meta[2 + 2 * per + micro * per + at] for at in range(per)]
    return core, micro, begin, ends, groups


def long_rows(values, half, small):
    return jnp.concatenate([values[0:half], values[half + small : 2 * half + small]], 0)


def small_rows(values, half, small):
    return jnp.concatenate([values[half : half + small], values[2 * half + small :]], 0)


def q_starts(half, small, step):
    return [at for base in (0, half + small) for at in range(base, base + half, step)]


def segment_of(place, ends):
    return sum((place >= end).astype(i32) for end in ends)


def small_same(meta, per, small):
    core, _, begin, ends, _ = facts(meta, per)

    def segments(shape, axis):
        at = lax.broadcasted_iota(i32, shape, axis)
        which = jnp.where(at < small, core, 1 - core)
        place = begin + LONGEST + which * small + jnp.where(at < small, at, at - small)
        total = LONGEST + 2 * small
        return segment_of(jnp.where(place >= total, place - total, place), ends)

    count = 2 * small
    return segments((count, count), 0) == segments((count, count), 1)


def row_places(meta, per, half, small, axis):
    core, _, begin, _, _ = facts(meta, per)
    own = half + small
    at = lax.broadcasted_iota(i32, (2 * own, 1) if axis == 0 else (1, 2 * own), axis)
    which = jnp.where(at < own, core, 1 - core)
    at = jnp.where(at < own, at, at - own)
    place = begin + jnp.where(at < half, which * half + at, LONGEST + which * small + at - half)
    total = LONGEST + 2 * small
    return jnp.where(place >= total, place - total, place)


def row_segments(meta, per, half, small):
    return segment_of(row_places(meta, per, half, small, 0), facts(meta, per)[3])


def chunks(rows):
    step = rows // PIECES
    return [slice(at, at + step) for at in range(0, rows, step)]


PIECES = 4


def both(refs, rows):
    at = rows.start // (rows.stop - rows.start)
    there = (at + PIECES // 2) % PIECES
    return getattr(refs, f"mine{at}")[...].astype(f32) + getattr(refs, f"came{there}")[...].astype(f32)


def parts_in(norm):
    made = {f"mine{at}": (NEAR, value) for at, value in enumerate(norm.mine)}
    return made | {f"came{at}": (NEAR, value) for at, value in enumerate(norm.came)}


def parts_out(rows, model):
    return {f"mine{at}": (NEAR, (rows // PIECES, model), bf16) for at in range(PIECES)}


def parts_of(got):
    return [getattr(got, f"mine{at}") for at in range(PIECES)]


def norm_into(refs, line):
    vecs = refs.vecs[8 * line : 8 * line + 8]
    for rows in chunks(refs.low.held.shape[0]):
        value = refs.base[rows].astype(f32) + (both(refs, rows) + vecs[0:1])
        centered = value - jnp.mean(value, -1, keepdims=True)
        inv_std = lax.rsqrt(jnp.mean(centered * centered, -1, keepdims=True) + LN_EPS)
        normed = centered * inv_std
        made = normed * vecs[1:2] + vecs[2:3]
        if hasattr(refs, "y"):
            refs.y[rows] = made
        refs.low[rows] = made.astype(bf16)
        refs.n[rows] = normed.astype(bf16)
        refs.r[rows] = inv_std
    for ref in (refs.low, refs.n, refs.r):
        ref.flush()
    if hasattr(refs, "y"):
        refs.y.flush()


def norm_results(rows, width, keep=True):
    made = dict(
        low=(FAR, (rows, width), bf16),
        n=(FAR, (rows, width), bf16),
        r=(FAR, (rows, 1), f32),
    )
    return made | (dict(y=(FAR, (rows, width), f32)) if keep else {})


def norm_back_into(refs, line):
    gain = refs.vecs[8 * line : 8 * line + 8][1:2]
    sums = None
    rows_all = refs.n.held.shape[0]
    for rows in chunks(rows_all):
        if hasattr(refs, "grad"):
            grad = refs.grad[rows]
        else:
            grad = refs.base[rows] + both(refs, rows)
        normed = refs.n[rows].astype(f32)
        inner = grad * gain
        made = refs.r[rows] * (
            inner
            - jnp.mean(inner, -1, keepdims=True)
            - normed * jnp.mean(inner * normed, -1, keepdims=True)
        )
        low = made.astype(bf16)
        refs.g[rows] = made
        refs.low[rows] = low
        lines = [
            jnp.sum(value, 0, keepdims=True) for value in (grad * normed, grad, low.astype(f32))
        ]
        sums = lines if sums is None else [a + b for a, b in zip(sums, lines)]
    refs.g.flush()
    refs.low.flush()
    for at, value in enumerate(sums):
        refs.sums[at : at + 1] = value
    refs.sums[3:] = jnp.zeros((5, sums[0].shape[1]), f32)
    refs.sums.flush()


def heads_into(refs, meta, per, line, heads, half, small):
    width = heads * HEAD

    bias = refs.units[line : line + 1]
    made = nt(refs.low[...], refs.w_qkv[...])
    refs.q[...] = (made[:, :width] + bias[:, :width]).astype(bf16)
    refs.k[...] = made[:, width : 2 * width].astype(bf16)
    refs.v[...] = (made[:, 2 * width :] + bias[:, width : 2 * width]).astype(bf16)
    for ref in (refs.q, refs.k, refs.v):
        ref.flush()
    scale = HEAD**-0.5
    same = small_same(meta, per, small)
    a_out, lse_out = refs.a, refs.lse
    for head in range(heads):
        cols = slice(head * HEAD, (head + 1) * HEAD)
        line = slice(head, head + 1)
        k_head = refs.k[:, cols]
        v_head = refs.v[:, cols]
        q_head = refs.q[:, cols] * scale
        k_long = long_rows(k_head, half, small)
        v_long_t = long_rows(v_head, half, small).T
        for at in q_starts(half, small, Q_ROWS):
            scores = nt(k_long, q_head[at : at + Q_ROWS])
            top = jnp.max(scores, 0, keepdims=True)
            probs = jnp.exp(scores - top)
            mass = jnp.sum(probs, 0, keepdims=True)
            out = nn(v_long_t, probs.astype(bf16)) / mass
            a_out[at : at + Q_ROWS, cols] = out.T.astype(bf16)
            lse_out[line, at : at + Q_ROWS] = top + jnp.log(mass)
        scores = nt(small_rows(k_head, half, small), small_rows(q_head, half, small))
        scores = jnp.where(same, scores, MASKED)
        top = jnp.max(scores, 0, keepdims=True)
        probs = jnp.exp(scores - top)
        mass = jnp.sum(probs, 0, keepdims=True)
        out = nn(small_rows(v_head, half, small).T, probs.astype(bf16)) / mass
        out = out.T.astype(bf16)
        a_out[half : half + small, cols] = out[:small]
        a_out[2 * half + small :, cols] = out[small:]
        lse = top + jnp.log(mass)
        lse_out[line, half : half + small] = lse[:, :small]
        lse_out[line, 2 * half + small :] = lse[:, small:]
    a_out.flush()
    lse_out.flush()


def heads_results(rows, width):
    made = (FAR, (rows, width), bf16)
    return dict(q=made, k=made, v=made, a=made, lse=(FAR, (8, rows), f32))


def attend_first(meta, per, small, line, x_all, norm, w_qkv, layer, units):
    width = w_qkv.shape[1] // 3
    heads = width // HEAD
    rows, model = (x_all if norm is None else norm.base).shape
    half = rows // 2 - small
    operands = dict(meta=(SCALAR, meta))
    results = {}
    if norm is None:
        operands |= dict(low=(NEAR, x_all))
    else:
        operands |= parts_in(norm) | dict(base=(FAR, norm.base), vecs=(FAR, norm.vecs))
        results = norm_results(rows, model)
    operands |= dict(w_qkv=(FAR, w_qkv, layer), units=(FAR, units))

    def body(refs):
        if norm is not None:
            norm_into(refs, norm.line)
        heads_into(refs, refs.meta, per, line, heads, half, small)

    return run("attend", body, operands, results | heads_results(rows, width))


def attend_second(meta, per, small, line, x_all, w_qkv, units, a_own, w_out_own, layer, w_out_par):
    width = w_qkv.shape[0] // 3
    heads = width // HEAD
    rows, model = x_all.shape
    half = rows // 2 - small

    def body(refs):
        heads_into(refs, refs.meta, per, line, heads, half, small)

        for at, part in enumerate(chunks(rows)):
            made = nn(refs.a_own[part], refs.wo_own[...]) + nn(refs.a[part], refs.wo_par[...])
            getattr(refs, f"mine{at}")[...] = made.astype(bf16)

    operands = dict(
        meta=(SCALAR, meta),
        low=(FAR, x_all),
        w_qkv=(FAR, w_qkv),
        units=(FAR, units),
        a_own=(FAR, a_own),
        wo_own=(FAR, w_out_own, layer),
        wo_par=(FAR, w_out_par),
    )
    return run("attend", body, operands, heads_results(rows, width) | parts_out(rows, model))


def ffn_into(refs, line):
    bias = refs.units[line : line + 1]
    rows_all = refs.hidden.held.shape[0]
    for rows in chunks(rows_all):
        hidden, slope = gelu_pair(nn(refs.low[rows], refs.w_up[...]) + bias)
        refs.hidden[rows] = hidden.astype(bf16)
        refs.slope[rows] = slope.astype(bf16)
        if rows.stop * 2 % rows_all == 0:
            refs.hidden.flush(rows.stop * 2 // rows_all - 1)
            refs.slope.flush(rows.stop * 2 // rows_all - 1)


def hidden_results(rows, units):
    made = ([(0, rows // 2), (rows // 2, rows)], (rows, units), bf16)
    return dict(hidden=made, slope=made)


def ffn_first(meta, line, norm, w_up, layer, units):
    rows, model = norm.base.shape

    def body(refs):
        norm_into(refs, norm.line)
        ffn_into(refs, line)

    operands = dict(meta=(SCALAR, meta)) | parts_in(norm)
    operands |= dict(
        base=(FAR, norm.base), vecs=(FAR, norm.vecs), w_up=(FAR, w_up, layer), units=(FAR, units)
    )
    return run("ffn", body, operands, norm_results(rows, model) | hidden_results(rows, w_up.shape[2]))


def ffn_second(meta, line, y_low, w_up, units, hidden_own, w_down_own, layer, w_down_par):
    rows, model = y_low.shape

    def body(refs):
        ffn_into(refs, line)
        for at, part in enumerate(chunks(rows)):
            made = nn(refs.hidden_own[part], refs.wd_own[...]) + nn(refs.hidden[part], refs.wd_par[...])
            getattr(refs, f"mine{at}")[...] = made.astype(bf16)

    operands = dict(
        meta=(SCALAR, meta),
        low=(FAR, y_low),
        w_up=w_up,
        units=(FAR, units),
        hidden_own=(FAR, hidden_own),
        wd_own=(FAR, w_down_own, layer),
        wd_par=w_down_par,
    )
    results = hidden_results(rows, w_up[1].shape[-1]) | parts_out(rows, model)
    return run("ffn", body, operands, results)


def norm_back_results(rows, width):
    return dict(
        g=(FAR, (rows, width), f32), low=(FAR, (rows, width), bf16), sums=(FAR, (8, width), f32)
    )


def ffn_back(meta, norm, kept, y_low, w_up, w_down, extra, other):
    rows, model = y_low.shape
    units = w_up[1].shape[-1]
    count = units + model + (0 if extra is None else extra.shape[0])
    first = norm is not None
    operands = dict(meta=(SCALAR, meta))
    operands |= norm.operands if first else dict(low=(FAR, other.low))
    operands |= dict(w_down=w_down, slope=(FAR, kept.slope), hidden=(FAR, kept.hidden), y=(FAR, y_low))
    if extra is not None:
        operands |= dict(extra=(FAR, extra))
    results = dict(
        grads=([(0, units), (units, count)], (count, model), bf16), line=(FAR, (8, units), f32)
    )
    if first:
        results |= norm_back_results(rows, model) | dict(pre=(FAR, (rows, units), bf16))
    else:
        operands |= dict(w_up=w_up, pre_other=(FAR, other.pre), w_up_other=other.w_up)
        results |= parts_out(rows, model)

    def body(refs):
        if first:
            norm_back_into(refs, norm.line)
            pre_ref = refs.pre
        else:
            pre_ref = refs.scratch[0]

        @stage
        def _():
            total = None
            for at in chunks(rows):
                pre = (refs.slope[at].astype(f32) * nt(refs.low[at], refs.w_down[...])).astype(bf16)
                pre_ref[at] = pre
                line = jnp.sum(pre.astype(f32), 0, keepdims=True)
                total = line if total is None else total + line
            if first:
                pre_ref.flush()
            refs.line[0:1] = total
            refs.line[1:] = jnp.zeros((7, units), f32)
            refs.line.flush()

        @stage
        def _():
            refs.grads[:units] = tn(refs.hidden[...], refs.low[...]).astype(bf16)
            refs.grads.flush(0)

        @stage
        def _():
            refs.grads[units : units + model] = tn(refs.y[...], pre_ref[...]).astype(bf16)
            if extra is not None:
                refs.grads[units + model :] = refs.extra[...]
            refs.grads.flush(1)

        if not first:

            @stage
            def _():
                for at, part in enumerate(chunks(rows)):
                    made = nt(pre_ref[part], refs.w_up[...]) + nt(refs.pre_other[part], refs.w_up_other[...])
                    getattr(refs, f"mine{at}")[...] = made.astype(bf16)

    scratch = () if first else (pltpu.VMEM((rows, units), bf16),)
    return run("ffn_back", body, operands, results, scratch=scratch)


def attend_back(meta, per, small, norm, kept, x_all, w_qkv, w_out, other, last):
    rows, model = x_all.shape
    width = w_out[1].shape[-2]
    half = rows // 2 - small
    first = norm is not None
    scale = HEAD**-0.5
    operands = dict(meta=(SCALAR, meta))
    operands |= norm.operands if first else dict(low=(FAR, other.low))
    operands |= dict(
        w_out=w_out,
        a=(FAR, kept.a),
        k=(FAR, kept.k),
        q=(FAR, kept.q),
        lse=(FAR, kept.lse),
        v=(FAR, kept.v),
        x=(FAR, x_all),
    )
    results = dict(
        grads=([(0, 3 * width), (3 * width, 4 * width)], (4 * width, model), bf16),
        line=(FAR, (8, 3 * width), f32),
    )
    if first:
        results |= norm_back_results(rows, model) | dict(g_qkv=(FAR, (rows, 3 * width), bf16))
    else:
        operands |= dict(w_qkv=w_qkv, g_other=(FAR, other.g_qkv), w_other=(FAR, other.w_qkv))
        if last:
            operands |= dict(g_norm=(FAR, other.g))
            results |= dict(own=(NEAR, (rows // 2, model), f32), away=(NEAR, (rows // 2, model), bf16))
        else:
            results |= parts_out(rows, model)
    scratch = [
        pltpu.VMEM((rows, width), bf16),
        pltpu.VMEM((2 * half, HEAD), f32),
        pltpu.VMEM((2 * half, HEAD), f32),
    ]
    if not first:
        scratch.append(pltpu.VMEM((rows, 3 * width), bf16))

    def body(refs):
        if first:
            norm_back_into(refs, norm.line)
            g_ref = refs.g_qkv
        else:
            g_ref = refs.scratch[3]
        da_ref, dv_sum, dk_sum = refs.scratch[:3]

        low = refs.low[...]
        da_ref[...] = nt(low, refs.w_out[...]).astype(bf16)
        refs.grads[3 * width :] = tn(refs.a[...], low).astype(bf16)
        refs.grads.flush(1)

        same = small_same(refs.meta, per, small)

        ones = jnp.ones((8, HEAD), f32)
        for head in range(width // HEAD):
            cols = slice(head * HEAD, (head + 1) * HEAD)
            line = slice(head, head + 1)
            k_head = refs.k[:, cols]
            v_head = refs.v[:, cols]
            q_head = refs.q[:, cols] * scale
            da_head = da_ref[:, cols]
            inner = da_head.astype(f32) * refs.a[:, cols].astype(f32)
            delta = exact(ones, inner, ((1,), (1,)))[0:1]
            k_long = long_rows(k_head, half, small)
            v_long = long_rows(v_head, half, small)
            k_long_t = (k_long * scale).T
            for count, at in enumerate(q_starts(half, small, Q_ROWS)):
                here = slice(at, at + Q_ROWS)
                q_blk = q_head[here]
                da_blk = da_head[here]
                probs = jnp.exp(nt(k_long, q_blk) - refs.lse[line, here])
                g_probs = nt(v_long, da_blk)
                g_scores = (probs * (g_probs - delta[:, here])).astype(bf16)
                g_v = nn(probs.astype(bf16), da_blk)
                g_k = nn(g_scores, q_blk)
                if count == 0:
                    dv_sum[...] = g_v
                    dk_sum[...] = g_k
                else:
                    dv_sum[...] += g_v
                    dk_sum[...] += g_k
                g_ref[here, cols] = nn(k_long_t, g_scores).T.astype(bf16)
            k_cols = slice(width + head * HEAD, width + (head + 1) * HEAD)
            v_cols = slice(2 * width + head * HEAD, 2 * width + (head + 1) * HEAD)
            for part, base in enumerate((0, half + small)):
                g_ref[base : base + half, k_cols] = dk_sum[part * half : (part + 1) * half].astype(bf16)
                g_ref[base : base + half, v_cols] = dv_sum[part * half : (part + 1) * half].astype(bf16)
            k_small = small_rows(k_head, half, small)
            q_small = small_rows(q_head, half, small)
            da_small = small_rows(da_head, half, small)
            lse = jnp.concatenate(
                [refs.lse[line, half : half + small], refs.lse[line, 2 * half + small :]], 1
            )
            delta = jnp.concatenate([delta[:, half : half + small], delta[:, 2 * half + small :]], 1)
            probs = jnp.exp(jnp.where(same, nt(k_small, q_small), MASKED) - lse)
            g_probs = nt(small_rows(v_head, half, small), da_small)
            g_scores = (probs * (g_probs - delta)).astype(bf16)
            for where, made in (
                (cols, nn((k_small * scale).T, g_scores).T),
                (k_cols, nn(g_scores, q_small)),
                (v_cols, nn(probs.astype(bf16), da_small)),
            ):
                g_ref[half : half + small, where] = made[:small].astype(bf16)
                g_ref[2 * half + small :, where] = made[small:].astype(bf16)

        if first:
            g_ref.flush()
        g_all = g_ref[...]
        refs.grads[: 3 * width] = tn(g_all, refs.x[...]).astype(bf16)
        refs.grads.flush(0)
        refs.line[0:1] = jnp.sum(g_all.astype(f32), 0, keepdims=True)
        refs.line[1:] = jnp.zeros((7, 3 * width), f32)
        refs.line.flush()

        if not first:
            core = facts(refs.meta, per)[0]
            place = row_places(refs.meta, per, half, small, 1)

            made = nn(g_ref[...], refs.w_qkv[...]) + nn(refs.g_other[...], refs.w_other[...])
            if last:
                own = rows // 2
                made = made + jnp.concatenate([refs.g_norm[:own], jnp.zeros((own, model), f32)], 0)
                high = made.astype(bf16)
                rest = (made - high.astype(f32)).astype(bf16)
                at = lax.broadcasted_iota(i32, (own, rows), 0)
                pick = (place == core * own + at).astype(bf16)
                refs.own[...] = nn(pick, high) + nn(pick, rest)
                refs.away[...] = nn((place == (1 - core) * own + at).astype(bf16), high).astype(bf16)
            else:
                for at, part in enumerate(chunks(rows)):
                    getattr(refs, f"mine{at}")[...] = made[part].astype(bf16)

    return run("attend_back", body, operands, results, scratch=scratch)


def halve(place, value, other):
    rows, width = value.shape[0] // 2, value.shape[1]
    kind = value.dtype
    if rows % 16:

        def take(which):
            return sum(
                lax.dynamic_slice_in_dim(part, which * rows, rows, 0).astype(f32) for part in (value, other)
            ).astype(kind)

        return take(place[0]), take(1 - place[0])

    def body(refs):
        place = refs.place[0]
        for out, which in ((refs.sent, 1 - place), (refs.kept, place)):
            part = pl.ds(pl.multiple_of(which * rows, 16), rows)
            out[...] = (refs.value[part].astype(f32) + refs.other[part].astype(f32)).astype(kind)

    made = (NEAR, (rows, width), kind)
    got = run(
        "halve",
        body,
        dict(place=(SCALAR, place), value=(NEAR, value), other=(NEAR, other)),
        dict(kept=made, sent=made),
    )
    return got.kept, got.sent


def join(place, mine, other):
    rows, width = mine.shape
    if rows % 16:
        return jnp.where(place[0] == 1, jnp.concatenate([other, mine], 0), jnp.concatenate([mine, other], 0))

    def body(refs):
        place = refs.place[0]
        refs.out[pl.ds(pl.multiple_of(place * rows, 16), rows)] = refs.mine[...]
        refs.out[pl.ds(pl.multiple_of((1 - place) * rows, 16), rows)] = refs.other[...]

    return run(
        "join",
        body,
        dict(place=(SCALAR, place), mine=(NEAR, mine), other=(NEAR, other)),
        dict(out=(NEAR, (2 * rows, width), mine.dtype)),
    ).out


def slices(meta, weights, strips, strip_rows):
    given = [*weights, *strips]
    model = given[-1][0].shape[2]

    def body(meta_ref, *refs):
        sems, outs = refs[-1], refs[len(given) : -1]
        copies = []
        for at, (_, layer) in enumerate(given):
            if at < len(weights):
                copies.append((refs[at].at[layer], outs[at]))
            else:
                rows = pl.ds(pl.multiple_of(meta_ref[0] * strip_rows, 16), strip_rows)
                part = pl.ds((at - len(weights)) * strip_rows, strip_rows)
                copies.append((refs[at].at[layer, rows], outs[-1].at[part]))
        copies = [pltpu.make_async_copy(*pair, sems.at[at]) for at, pair in enumerate(copies)]
        for copy in copies:
            copy.start()
        for copy in copies:
            copy.wait()

    made = [pltpu.VMEM(array.shape[1:], array.dtype) for array, _ in weights]
    made += [pltpu.VMEM((len(strips) * strip_rows, model), bf16)] if strips else []
    return pl.pallas_call(
        body,
        out_shape=tuple(made),
        in_specs=[SMEM] + [HBM] * len(given),
        out_specs=(VMEM,) * len(made),
        scratch_shapes=[pltpu.SemaphoreType.DMA((len(given),))],
        cost_estimate=pl.CostEstimate(flops=COST, transcendentals=0, bytes_accessed=0),
        name="slices",
    )(meta, *[pltpu.with_memory_space_constraint(array, pltpu.HBM) for array, _ in given])


def gather_small(meta, per, b_out, b_down, ln_gain, ln_shift, b_up, b_qv, queries):
    layers, units = b_up.shape
    model = b_out.shape[1]
    width = b_qv.shape[2]
    q_group, q_piece, dim = queries.shape
    q_rows = q_group * q_piece

    def body(meta, bo_ref, bd_ref, gain_ref, shift_ref, bu_ref, bqv_ref, q_ref, vec_out, line_out, carried_out):
        vec_out[...] = jnp.zeros(vec_out.shape, f32)
        line_out[...] = jnp.zeros(line_out.shape, f32)
        for layer in range(layers):
            for at, ref in ((0, bo_ref), (1, bd_ref)):
                first = 8 * (2 * layer + at)
                vec_out[first : first + 1] = ref[layer : layer + 1]
                vec_out[first + 1 : first + 2] = gain_ref[layer, at : at + 1]
                vec_out[first + 2 : first + 3] = shift_ref[layer, at : at + 1]
                line_out[2 * layer + 1 : 2 * layer + 2, at * width : (at + 1) * width] = bqv_ref[
                    layer, at : at + 1
                ]
            line_out[2 * layer : 2 * layer + 1] = bu_ref[layer : layer + 1].astype(f32)
        for at in range(q_group):
            carried_out[at * q_piece : (at + 1) * q_piece] = q_ref[at]
        lane = lax.broadcasted_iota(i32, (CARRIED - q_rows, dim), 1)
        row = lax.broadcasted_iota(i32, (CARRIED - q_rows, dim), 0)
        made = jnp.zeros((CARRIED - q_rows, dim), f32)
        for at in range(2 * per):
            made = jnp.where((lane == at) & (row == 0), meta[2 + 2 * per + at].astype(f32), made)
        carried_out[q_rows:] = made.astype(bf16)

    return pl.pallas_call(
        body,
        out_shape=(
            jax.ShapeDtypeStruct((16 * layers, model), f32),
            jax.ShapeDtypeStruct((-(-2 * layers // 8) * 8, units), f32),
            jax.ShapeDtypeStruct((CARRIED, dim), bf16),
        ),
        in_specs=[SMEM] + [VMEM] * 7,
        out_specs=(VMEM,) * 3,
        cost_estimate=pl.CostEstimate(flops=COST, transcendentals=0, bytes_accessed=0),
        name="gather_small",
    )(meta, b_out, b_down, ln_gain, ln_shift, b_up, b_qv, queries)


def turn(meta, per, small, x_own, x_other):
    own, model = x_own.shape
    rows = 2 * own

    def body(refs):
        core = facts(refs.meta, per)[0]
        place = row_places(refs.meta, per, own - small, small, 0)
        at = lax.broadcasted_iota(i32, (rows, own), 1)
        made = nn((place == core * own + at).astype(bf16), refs.mine[...])
        made = made + nn((place == (1 - core) * own + at).astype(bf16), refs.came[...])
        made = made.astype(bf16)
        refs.near[...] = made
        refs.low[...] = made
        refs.low.flush()

    operands = dict(meta=(SCALAR, meta), mine=(NEAR, x_own), came=(NEAR, x_other))
    results = dict(near=(NEAR, (rows, model), bf16), low=(FAR, (rows, model), bf16))
    return run("turn", body, operands, results)


CARRIED = 32


def query_of(at, q_group, q_piece):
    return at // q_piece % q_group


def score(meta, per, small, norm, w_proj, carried, q_group, q_piece, n_mp):
    rows, model = norm.base.shape
    half = rows // 2 - small
    dim = w_proj.shape[1]
    q_rows = q_group * q_piece
    q_tok = q_rows * n_mp
    count = per * q_tok
    n_dp = carried.shape[0] // (n_mp * CARRIED)

    def body(refs):
        norm_into(refs, norm.line)
        groups = facts(refs.meta, per)[4]
        for at in range(per):
            for piece in range(n_mp):
                side = piece % 2 * 2 + piece // 2
                source = pl.multiple_of((side * n_dp + groups[at]) * CARRIED, CARRIED)
                first = at * q_tok + piece * q_rows
                refs.flat_q[first : first + q_rows] = refs.carried[pl.ds(source, q_rows)]
        emb = nn(refs.low[...], refs.w_proj[...])
        unit = emb * lax.rsqrt(jnp.sum(emb * emb, -1, keepdims=True) + UNIT_EPS)
        segment = row_segments(refs.meta, per, half, small)
        owner = lax.broadcasted_iota(i32, (rows, count), 1) // q_tok == segment
        similar = nt(unit.astype(bf16), refs.flat_q[...])
        terms = jnp.where(owner, jnp.exp(SHARP * (similar - 1.0)), 0.0)
        totals = jnp.sum(terms, 0, keepdims=True)
        refs.totals[...] = jnp.broadcast_to(totals, (8, count))
        _, micro, _, _, _ = facts(refs.meta, per)
        slot = (refs.meta[0] * 2 + micro) * per
        lane = lax.broadcasted_iota(i32, (8, count), 1)
        length = jnp.zeros((8, count), f32)
        for at in range(per):
            size = jnp.full((8, count), refs.meta[2 + micro * per + at].astype(f32))
            length = jnp.where(lane // q_tok == at, size, length)
        term = (jnp.log(jnp.broadcast_to(totals, (8, count))) - jnp.log(length)) / SHARP + 1.0
        row = lax.broadcasted_iota(i32, (8, count), 0)
        term = jnp.where(query_of(lane, q_group, q_piece) == row, term, 0.0)
        n_pass = refs.logits.shape[1]
        target = lax.broadcasted_iota(i32, (count, n_pass), 1)
        source = lax.broadcasted_iota(i32, (count, n_pass), 0)
        pick = (source // q_tok + slot == target).astype(f32)
        refs.logits[...] = exact(term, pick) / TEMPER

    n_pass = carried.shape[0] // (n_mp * CARRIED) * 2 * per
    operands = dict(meta=(SCALAR, meta)) | parts_in(norm)
    operands |= dict(
        base=(FAR, norm.base),
        vecs=(FAR, norm.vecs),
        carried=(NEAR, carried),
        w_proj=(FAR, w_proj),
    )
    results = norm_results(rows, model, keep=False) | dict(
        flat_q=(NEAR, (count, dim), bf16),
        totals=(NEAR, (8, count), f32),
        logits=(NEAR, (8, n_pass), f32),
    )
    return run("score", body, operands, results)


def loss_back(meta, per, small, logits, groups, targets, totals, flat_q, final, w_proj, q_group, q_piece, n_mp):
    n_dp, n_pass = targets.shape[1], logits.shape[1]
    rows, model = final.shape
    half = rows // 2 - small
    dim = w_proj.shape[1]
    q_rows = q_group * q_piece
    q_tok = q_rows * n_mp
    count = per * q_tok
    held = n_dp * q_rows * (n_mp // 2)

    def body(refs):
        meta = refs.meta
        core, micro, _, _, own_groups = facts(meta, per)
        member = refs.groups[...] == lax.broadcasted_iota(i32, (n_dp, n_pass), 0)
        lane = lax.broadcasted_iota(i32, (n_dp, n_pass), 1)
        g_rows = []
        for query in range(q_group):
            logit = refs.logits[query : query + 1]
            spread = jnp.where(member, logit, FLOOR)
            top = jnp.max(spread, 1, keepdims=True)
            mass = jnp.sum(jnp.where(member, jnp.exp(spread - top), 0.0), 1, keepdims=True)
            lse = top + jnp.log(mass)
            hit = lane == refs.targets[query]
            refs.loss[query] = lse - jnp.sum(jnp.where(hit, logit, 0.0), 1, keepdims=True)
            lse_pass = jnp.sum(jnp.where(member, lse, 0.0), 0, keepdims=True)
            hits = jnp.sum(jnp.where(hit & member, 1.0, 0.0), 0, keepdims=True)
            g_rows.append(jnp.exp(logit - lse_pass) - hits)
        g_logit = jnp.concatenate(g_rows + [jnp.zeros((8 - q_group, n_pass), f32)], 0)
        slot = (meta[0] * 2 + micro) * per
        lane = lax.broadcasted_iota(i32, (n_pass, count), 0)
        at = lax.broadcasted_iota(i32, (n_pass, count), 1)
        wide = exact(g_logit, (at // q_tok + slot == lane).astype(f32))
        at = lax.broadcasted_iota(i32, (8, count), 1)
        row = lax.broadcasted_iota(i32, (8, count), 0)
        wide = jnp.where(query_of(at, q_group, q_piece) == row, wide, 0.0)
        wide = jnp.sum(wide, 0, keepdims=True)
        g_total = (wide / TEMPER) / (SHARP * refs.totals[0:1])
        low = refs.final[...]
        emb = nn(low, refs.w_proj[...])
        scale = lax.rsqrt(jnp.sum(emb * emb, -1, keepdims=True) + UNIT_EPS)
        unit = emb * scale
        unit_low = unit.astype(bf16)
        segment = row_segments(meta, per, half, small)
        owner = lax.broadcasted_iota(i32, (rows, count), 1) // q_tok == segment
        similar = nt(unit_low, refs.flat_q[...])
        terms = jnp.where(owner, jnp.exp(SHARP * (similar - 1.0)), 0.0)
        g_sim = (SHARP * terms * g_total).astype(bf16)
        g_unit = nn(g_sim, refs.flat_q[...])
        g_emb = scale * (g_unit - unit * jnp.sum(g_unit * unit, -1, keepdims=True))
        g_emb = g_emb.astype(bf16)
        refs.grad[...] = nt(g_emb, refs.w_proj[...])
        refs.proj[...] = tn(g_emb, low).astype(bf16)
        g_picked = tn(g_sim, unit_low)
        row = lax.broadcasted_iota(i32, (held, count), 0)
        source = lax.broadcasted_iota(i32, (held, count), 1)
        group = row // q_rows % n_dp
        piece = row // (q_rows * n_dp) * 2 + core
        want = piece * q_rows + row % q_rows
        line = lax.broadcasted_iota(i32, (1, count), 1) // q_tok
        source_group = jnp.zeros((1, count), i32)
        for passage in range(per):
            source_group = jnp.where(line == passage, own_groups[passage], source_group)
        pick = ((source % q_tok == want) & (source_group == group)).astype(f32)
        refs.queries[...] = exact(pick, g_picked)

    operands = dict(
        meta=(SCALAR, meta),
        logits=(NEAR, logits),
        groups=(NEAR, groups),
        targets=(NEAR, targets),
        totals=(NEAR, totals),
        flat_q=(NEAR, flat_q),
        final=(FAR, final),
        w_proj=(FAR, w_proj),
    )
    results = dict(
        loss=(NEAR, (q_group, n_dp, 1), f32),
        queries=(NEAR, (held, dim), f32),
        proj=(NEAR, (dim, model), bf16),
        grad=(NEAR, (rows, model), f32),
    )
    return run("loss_back", body, operands, results)


def pack(meta, sums, own, par):
    model = sums[0].shape[1]
    first = 8 * len(sums)
    rows = first + -(-2 * len(own) // 8) * 8
    operands = dict(meta=(SCALAR, meta)) | {f"sum{at}": (FAR, value) for at, value in enumerate(sums)}
    for layer, pairs in enumerate(zip(own, par)):
        for side, pair in enumerate(pairs):
            for at, value in enumerate(pair):
                operands[f"line{layer}{side}{at}"] = (FAR, value)

    def body(refs):
        for side, out in enumerate((refs.own, refs.par)):
            out[first:] = jnp.zeros((rows - first, model), f32)
            for at in range(len(sums)):
                out[8 * at : 8 * at + 8] = getattr(refs, f"sum{at}")[...]
            for layer in range(len(own)):
                for at in range(2):
                    value = getattr(refs, f"line{layer}{side}{at}")
                    row = first + 2 * layer + at
                    out[row : row + 1, : value.held.shape[1]] = value[0:1]

    made = (NEAR, (rows, model), f32)
    got = run("pack", body, operands, dict(own=made, par=made))
    return got.own, got.par


def quarters(place, value, other):
    rows, width = value.shape[0] // 4, value.shape[1]

    def body(refs):
        for at in (1, 2, 3, 0):
            part = pl.ds(pl.multiple_of((refs.place[0] ^ at) * rows, 16), rows)
            made = refs.value[part].astype(f32) + refs.other[part].astype(f32)
            getattr(refs, f"part{at}")[...] = made.astype(value.dtype)

    operands = dict(place=(SCALAR, place), value=(NEAR, value), other=(NEAR, other))
    results = {f"part{at}": (NEAR, (rows, width), value.dtype) for at in range(4)}
    got = run("quarters", body, operands, results)
    return [getattr(got, f"part{at}") for at in range(4)]


def join_quarters(place, *parts):
    rows, width = parts[0].shape

    def body(refs):
        for at in range(4):
            part = pl.ds(pl.multiple_of((refs.place[0] ^ at) * rows, 16), rows)
            refs.out[part] = getattr(refs, f"part{at}")[...]

    operands = dict(place=(SCALAR, place)) | {f"part{at}": (NEAR, part) for at, part in enumerate(parts)}
    return run("join", body, operands, dict(out=(NEAR, (4 * rows, width), parts[0].dtype))).out


def store(layer, layers, parts, before):
    count = len(parts)
    model = parts[0][0].shape[1]
    sources = []
    for array, _, _ in parts:
        if all(array is not other for other in sources):
            sources.append(array)

    def body(*refs):
        outs = refs[len(sources) + (count if before else 0) :][:count]
        held, sems = refs[-1 - count : -1], refs[-1]
        for at, (array, first, rows) in enumerate(parts):
            source = [ref for ref, given in zip(refs, sources) if given is array][0]
            held[at][...] = source[first : first + rows].astype(f32)
            pltpu.make_async_copy(held[at], outs[at].at[layer], sems.at[at]).start()
        for at in range(count):
            pltpu.make_async_copy(held[at], outs[at].at[layer], sems.at[at]).wait()

    given = [pltpu.with_memory_space_constraint(value, pltpu.VMEM) for value in sources]
    if before:
        given += [pltpu.with_memory_space_constraint(value, pltpu.HBM) for value in before]
    return pl.pallas_call(
        body,
        out_shape=tuple(pltpu.HBM((layers, rows, model), f32) for _, _, rows in parts),
        in_specs=[VMEM] * len(sources) + [HBM] * (count if before else 0),
        out_specs=(HBM,) * count,
        scratch_shapes=[pltpu.VMEM((rows, model), f32) for _, _, rows in parts]
        + [pltpu.SemaphoreType.DMA((count,))],
        input_output_aliases={len(sources) + at: at for at in range(count)} if before else {},
        compiler_params=pltpu.CompilerParams(vmem_limit_bytes=VMEM_LIMIT),
        cost_estimate=pl.CostEstimate(flops=COST, transcendentals=0, bytes_accessed=0),
        name="store",
    )(*given)


def add(*parts):
    def body(refs):
        total = sum(getattr(refs, f"part{at}")[...].astype(f32) for at in range(len(parts)))
        refs.out[...] = total.astype(parts[0].dtype)

    operands = {f"part{at}": (NEAR, part) for at, part in enumerate(parts)}
    return run("add", body, operands, dict(out=(NEAR, parts[0].shape, parts[0].dtype))).out


def on_device(
    passages_in,
    queries,
    w_qkv,
    b_qv,
    w_out,
    b_out,
    ln_gain,
    ln_shift,
    w_up,
    b_up,
    w_down,
    b_down,
    w_proj,
    lengths,
    passage_group,
    positive,
):
    n_mp = lax.axis_size("mp")
    n_dp = lax.axis_size("dp")
    own, model = passages_in.shape
    micro_count, per = lengths.shape
    tok_mb = own * n_mp // micro_count
    assert n_mp == 4 and micro_count == 2 and n_dp & (n_dp - 1) == 0
    layers = w_qkv.shape[0]
    width = w_qkv.shape[3]
    ff = w_up.shape[2]
    small = (tok_mb - LONGEST) // 2
    q_group, q_piece, dim = queries.shape
    q_rows = q_group * q_piece

    mp_here = lax.axis_index("mp")
    dp_here = lax.axis_index("dp")
    core, micro = mp_here % 2, mp_here // 2
    dp_bits = [1 << at for at in range(n_dp.bit_length() - 1)]

    def to_pair(value):
        return jax.tree.map(lambda part: lax.ppermute(part, "mp", [(at, at ^ 1) for at in range(n_mp)]), value)

    def to_x(value):
        return lax.ppermute(value, "mp", [(at, at ^ 2) for at in range(n_mp)])

    def to_dp(value, bit):
        return lax.ppermute(value, "dp", [(at, at ^ bit) for at in range(n_dp)])

    noted = []

    def here(value):
        return lax.optimization_barrier((value, noted[-1]))[0] if noted else value

    def note(value):
        noted.append(value)
        return value

    meta = jnp.concatenate(
        [jnp.stack([dp_here, mp_here]).astype(i32), lengths.reshape(-1), passage_group.reshape(-1)]
    )
    core_place, micro_place = core[None].astype(i32), micro[None].astype(i32)
    places = {bit: ((dp_here // bit) % 2)[None].astype(i32) for bit in dp_bits}

    w_qkv = w_qkv.transpose(0, 2, 3, 1).reshape(layers, 3 * width, model)
    x_other = to_pair(passages_in)
    strip_rows = model // n_dp

    def strips_of(meta, pairs):
        if strip_rows % 16 == 0:
            return slices(meta, [], pairs, strip_rows)[0]
        parts = [
            lax.dynamic_slice_in_dim(array[layer], dp_here * strip_rows, strip_rows, 0) for array, layer in pairs
        ]
        return jnp.concatenate(parts, 0)

    def gathered(strip):
        count = strip.shape[0] // strip_rows
        stack = lax.all_gather(strip, "dp", axis=0)
        if strip_rows % 16:
            parts = [stack[:, at * strip_rows : (at + 1) * strip_rows] for at in range(count)]
            return [(FAR, part.reshape(-1, model)) for part in parts]
        return [
            (FAR, stack, (slice(None), slice(at * strip_rows, (at + 1) * strip_rows))) for at in range(count)
        ]

    def after(value, first):
        return lax.optimization_barrier((value, first))[0]

    strip = strips_of(meta, [(w_up, 0), (w_down, 0)])
    strip_par = to_x(strip)
    vecs, lines, first_carried = gather_small(
        after(meta, strip), per, b_out, b_down, ln_gain, ln_shift, b_up, b_qv, queries
    )
    lines_par = to_x(lines)
    turned = turn(after(meta, lines), per, small, passages_in, x_other)
    sent = slices(after(meta, turned.low), [(w_qkv, 0), (w_out, 0)], [], strip_rows)
    w_par = [SimpleNamespace() for _ in range(layers)]
    w_par[0].up, w_par[0].down = gathered(after(strip_par, sent[0]))
    w_par[0].qkv, w_par[0].out = (to_x(after(value, lines_par)) for value in sent)

    def spread():
        value = first_carried
        steps = [((lambda v, bit=bit: to_dp(v, bit)), places[bit]) for bit in dp_bits]
        steps += [(to_x, micro_place), (to_pair, core_place)]
        for send, place in steps:
            other = send(value)
            yield
            value = note(join(here(place), value, other))
        yield value

    spreading, spread_out = spread(), []

    def spread_on():
        spread_out.append(next(spreading, None))

    spread_on()

    x_all, base, norm = turned.low, turned.low, None
    stored = []
    for layer in range(layers):
        par = w_par[layer]
        att_own = attend_first(
            here(meta), per, small, 2 * layer + 1, turned.near if norm is None else None, norm, w_qkv, layer, lines
        )
        note(att_own.lse)
        if layer == 0:
            spread_on()
        if norm is not None:
            x_all, base = att_own.low, att_own.y
        att_par = attend_second(
            here(meta), per, small, 2 * layer + 1, x_all, par.qkv, lines_par, att_own.a, w_out, layer, par.out
        )
        note(att_par.lse)
        if layer + 1 < layers:
            strip_par = to_x(strips_of(here(meta), [(w_up, layer + 1), (w_down, layer + 1)]))
        norm = SimpleNamespace(
            mine=parts_of(att_par), came=to_pair(parts_of(att_par)), base=base, vecs=vecs, line=2 * layer
        )
        spread_on()
        ffn_own = ffn_first(here(meta), 2 * layer, norm, w_up, layer, lines)
        note(ffn_own.r)
        if layer != 0:
            spread_on()
        if layer + 1 < layers:
            at = layer + 1
            w_par[at].up, w_par[at].down = gathered(here(strip_par))
            pieces = slices(here(meta), [(w_qkv, at), (w_out, at)], [], strip_rows)
            w_par[at].qkv, w_par[at].out = (to_x(value) for value in pieces)
        ffn_par = ffn_second(
            here(meta), 2 * layer, ffn_own.low, par.up, lines_par, ffn_own.hidden, w_down, layer, par.down
        )
        note(ffn_par.mine0)
        norm = SimpleNamespace(
            mine=parts_of(ffn_par),
            came=to_pair(parts_of(ffn_par)),
            base=ffn_own.y,
            vecs=vecs,
            line=2 * layer + 1,
        )
        if layer == 0:
            spread_on()
        stored.append([x_all, att_own, att_par, ffn_own, ffn_par])
    spread_out += list(spreading)
    carried = next(value for value in spread_out if value is not None)
    groups = carried.reshape(n_mp, n_dp, CARRIED, dim)[0, :, q_rows, : passage_group.size]
    groups = groups.reshape(1, -1).astype(i32)

    found = score(here(meta), per, small, norm, w_proj, carried, q_group, q_piece, n_mp)
    norms_after = [stored[layer][1] for layer in range(1, layers)] + [found]
    logits = found.logits
    logits = logits + to_x(logits)
    for bit in dp_bits:
        logits = logits + to_dp(logits, bit)
    back = loss_back(
        meta,
        per,
        small,
        logits,
        groups,
        positive.reshape(n_dp, q_group).T[:, :, None],
        found.totals,
        found.flat_q,
        found.low,
        w_proj,
        q_group,
        q_piece,
        n_mp,
    )
    note(back.grad)
    query_loss = lax.dynamic_index_in_dim(back.loss[:, :, 0], dp_here, 1, keepdims=False)

    def total(theirs):
        other = to_x(here(theirs))
        value = yield
        yield
        for bit in dp_bits:
            value, sent = halve(here(places[bit]), value, other)
            note(value)
            other = to_dp(sent, bit)
            yield
        value = note(add(here(value), other))
        for bit in reversed(dp_bits):
            other = to_dp(value, bit)
            yield
            value = note(join(here(places[bit]), value, other))
        yield value

    def total_early(theirs):
        other = to_x(here(theirs))
        value = yield
        yield
        value, sent = halve(here(places[1]), value, other)
        note(value)
        other = to_dp(sent, 1)
        yield
        value = note(add(here(value), other))
        value = lax.psum(value, "dp", axis_index_groups=[list(range(side, n_dp, 2)) for side in range(2)])
        yield
        value = note(here(value))
        yield
        value = here(value)
        other = to_dp(value, 1)
        yield
        yield note(join(here(places[1]), value, other))

    def query_sums():
        value = back.queries
        rows = value.shape[0] // 2
        other = to_x(lax.dynamic_slice_in_dim(value, (1 - micro) * rows, rows, 0))
        value = lax.dynamic_slice_in_dim(value, micro * rows, rows, 0)
        for bit in reversed(dp_bits):
            yield
            value, sent = halve(here(places[bit]), value, other)
            note(value)
            other = to_dp(sent, bit)
        yield
        yield note(add(here(value), other))

    queried = query_sums()
    next(queried)
    running = []

    def advance(which, count=1):
        for _ in range(count):
            got = next(running[which])
        return got

    finals = [None] * (2 * layers)
    rep_sums, own_sums, par_sums = [None] * (2 * layers), [None] * layers, [None] * layers
    grads = dict(grad=(NEAR, back.grad))
    for layer in reversed(range(layers)):
        x_all, att_own, att_par, ffn_own, ffn_par = stored[layer]
        par = w_par[layer]
        last = layer == layers - 1
        extra = back.proj if last else None

        def way(line, kept):
            rest = dict(n=(FAR, kept.n), r=(FAR, kept.r), vecs=(FAR, vecs))
            return SimpleNamespace(operands=grads | rest, line=line)

        got_par = ffn_back(
            here(meta),
            way(2 * layer + 1, norms_after[layer]),
            ffn_par,
            ffn_own.low,
            par.up,
            par.down,
            extra,
            None,
        )
        note(got_par.line)
        if last:
            next(queried)
        else:
            advance(0)
            advance(1)
        running.append((total_early if last else total)(got_par.grads))
        advance(-1)
        other = SimpleNamespace(low=got_par.low, pre=got_par.pre, w_up=par.up)
        got_own = ffn_back(
            here(meta), None, ffn_own, ffn_own.low, (FAR, w_up, layer), (FAR, w_down, layer), extra, other
        )
        note(got_own.line)
        running[-1].send(got_own.grads)
        rep_sums[2 * layer + 1] = got_par.sums
        bup = (got_own.line, got_par.line)
        exchanged = SimpleNamespace(mine=parts_of(got_own), came=to_pair(parts_of(got_own)))
        grads = parts_in(exchanged) | dict(base=(FAR, got_par.g))
        if last:
            next(queried)
        else:
            advance(1)
        got_par = attend_back(
            here(meta),
            per,
            small,
            way(2 * layer, ffn_own),
            att_par,
            x_all,
            (FAR, par.qkv),
            (FAR, par.out),
            None,
            False,
        )
        note(got_par.line)
        if not last:
            advance(2)
            advance(1)
            advance(0)
        running.append(total(got_par.grads))
        advance(-1)
        if last:
            next(queried)
        other = SimpleNamespace(low=got_par.low, g_qkv=got_par.g_qkv, w_qkv=par.qkv, g=got_par.g)
        got_own = attend_back(
            here(meta), per, small, None, att_own, x_all, (FAR, w_qkv, layer), (FAR, w_out, layer), other, layer == 0
        )
        note(got_own.line)
        running[-1].send(got_own.grads)
        rep_sums[2 * layer] = got_par.sums
        own_sums[layer] = (bup[0], got_own.line)
        par_sums[layer] = (bup[1], got_par.line)
        if layer:
            exchanged = SimpleNamespace(mine=parts_of(got_own), came=to_pair(parts_of(got_own)))
            grads = parts_in(exchanged) | dict(base=(FAR, got_par.g))
        if last:
            query_grad = [value for value in queried if value is not None][0].reshape(q_group, q_piece, dim)
            advance(0)
    input_grad = got_own.own + to_pair(got_own.away).astype(f32)

    count = 2 * layers * 8
    flat, flat_par = pack(here(meta), rep_sums, own_sums, par_sums)
    flat_other = to_x(flat_par)

    def flat_sums():
        value, other = flat, flat_other
        for bit in dp_bits:
            yield
            value = note(add(here(value), other))
            other = to_dp(value, bit)
        yield
        yield note(add(here(value), other))

    running.append(flat_sums())
    advance(-1)
    finals = [None] * len(running)
    turns = TURNS if n_dp == 8 and layers == 2 else []
    for which in turns:
        finals[which] = advance(which)
    for which in range(len(running)):
        for got in running[which]:
            finals[which] = got
    flat = finals.pop()
    made = None
    for layer in reversed(range(layers)):
        ffn_sums, att_sums = finals[2 * (layers - 1 - layer) : 2 * (layers - layer)]
        if layer == layers - 1:
            g_wproj = ffn_sums[ff + model :].astype(f32).T
        parts = [(att_sums, 0, 3 * width), (att_sums, 3 * width, width), (ffn_sums, ff, model), (ffn_sums, 0, ff)]
        made = store(layer, layers, parts, made)
    g_wqkv, g_wout, g_wup, g_wdown = made
    norms = flat[:count].reshape(layers, 2, 8, model)
    units = flat[count : count + 2 * layers].reshape(layers, 2, model)
    g_bqv = jnp.stack([units[:, 1, :width], units[:, 1, 2 * width : 3 * width]], 1)
    g_wqkv = g_wqkv.reshape(layers, 3, width, model).transpose(0, 3, 1, 2)
    return (
        query_loss,
        input_grad,
        query_grad,
        g_wqkv,
        g_bqv,
        g_wout,
        norms[:, 0, 2],
        norms[:, :, 0],
        norms[:, :, 1],
        g_wup,
        units[:, 0],
        g_wdown,
        norms[:, 1, 2],
        g_wproj,
    )


def solution(mesh):
    placed = (
        P(("dp", "mp"), None),
        P("dp", "mp", None),
        P(None, None, None, "mp"),
        P(None, None, "mp"),
        P(None, "mp", None),
        P(),
        P(),
        P(),
        P(None, None, "mp"),
        P(None, "mp"),
        P(None, "mp", None),
        P(),
        P(),
        P("dp", None),
        P("dp", None),
        P(),
    )
    return jax.shard_map(
        on_device,
        mesh=mesh,
        in_specs=placed,
        out_specs=(
            P("dp"),
            P(("dp", "mp"), None),
            P("dp", "mp", None),
            P(None, None, None, "mp"),
            P(None, None, "mp"),
            P(None, "mp", None),
            P(),
            P(),
            P(),
            P(None, None, "mp"),
            P(None, "mp"),
            P(None, "mp", None),
            P(),
            P(),
        ),
        check_vma=False,
    )
```
